128 devices in a mesh: section: 2 (over x_lo), dp: 16 (over x_hi, y, core), tensor: 4 (over z).
Axes of the slice: x: 4 (x_hi: 2, x_lo: 2; x = x_hi * 2 + x_lo), y: 4, z: 4, core: 2. Of those that a mesh axis runs over, the one named last changes fastest.
Arguments:
- tokens: bfloat16 [2, 4, 1, 1024, 768], P('section', None, None, 'dp'), may hold values from -6 to 6
- segments: int32 [2, 4, 1, 1024], replicated, may hold values from 0 to 3, as said below
- cotangent: bfloat16 [4, 1, 1024, 768], P(None, None, 'dp'), may hold values from -6 to 6
- attn_in: bfloat16 [2, 768, 3, 768], P('section', None, None, 'tensor'), may hold values from -0.21875 to 0.21875
- attn_out: bfloat16 [2, 768, 768], P('section', 'tensor'), may hold values from -2.5 to 2.5
- ffn_in: bfloat16 [2, 768, 3072], P('section', None, 'tensor'), may hold values from -0.21875 to 0.21875
- ffn_out: bfloat16 [2, 3072, 768], P('section', 'tensor'), may hold values from -0.109375 to 0.109375
- cross_proj: bfloat16 [2, 768, 2, 768], P('section', None, None, 'tensor'), may hold values from -1.6411581 to 1.6411581
- norms: float32 [2, 3, 2, 768], P('section'), may hold values from -0.76 to 1.46
Outputs:
- outputs: bfloat16 [2, 4, 1, 1024, 768], P('section', None, None, 'dp')
- token_grads: float32 [2, 4, 1, 1024, 768], P('section', None, None, 'dp')
- grad_attn_in: float32 [2, 768, 3, 768], P('section', None, None, 'tensor')
- grad_attn_out: float32 [2, 768, 768], P('section', 'tensor')
- grad_ffn_in: float32 [2, 768, 3072], P('section', None, 'tensor')
- grad_ffn_out: float32 [2, 3072, 768], P('section', 'tensor')
- grad_cross_proj: float32 [2, 768, 2, 768], P('section', None, None, 'tensor')
- grad_norms: float32 [2, 3, 2, 768], P('section')
The draws below stay inside these ranges and needn't reach their ends.
Inputs may be any that keep to these rules, and one draw needn't show every extreme that they name: `segments`: in each row the document numbers start at 0 and never fall, each of the 4 documents holds one position or more, so a source row and a target row hold the same document numbers.
All inputs are finite; a program needn't handle non-finite values.
Results may differ from the reference program's by a relative error of at most 0.035.
Values may be sent and summed in bfloat16 or wider, within the bound.
No kernel may reach another device: no remote copies, remote signals or barrier semaphores. Data moves between devices by JAX's collectives and lax.ppermute only.
A program may use at most 192 MiB of HBM per device.

```python
import math
import jax
import jax.numpy as jnp
from jax import lax

D = 768
FF = 3072
HEAD_DIM = 64
LEN = 1024
MICRO = 4
ROWS = 1
DOCS = 4
BLK = 64


def draw_segments(key, part):
    key = jax.random.fold_in(key, 11)
    row_total = 2 * MICRO * ROWS
    small_most = max((BLK - 1) // (DOCS - 1), 1)
    small_key, big_key = jax.random.split(key)
    small_lengths = jax.random.randint(small_key, (row_total, DOCS - 1), 1, small_most + 1)
    big_place = jax.random.randint(big_key, (row_total, 1), 0, DOCS)
    doc_place = lax.broadcasted_iota(jnp.int32, (row_total, DOCS), 1)
    zero_column = jnp.zeros((row_total, 1), jnp.int32)
    before_big = jnp.concatenate([small_lengths, zero_column], axis=1)
    after_big = jnp.concatenate([zero_column, small_lengths], axis=1)
    lengths = jnp.where(doc_place < big_place, before_big, jnp.where(doc_place > big_place, after_big, 0))
    lengths = jnp.where(doc_place == big_place, LEN - jnp.sum(lengths, axis=1, keepdims=True), lengths)
    doc_ends = jnp.cumsum(lengths, axis=1)[:, :DOCS - 1]
    positions = lax.broadcasted_iota(jnp.int32, (row_total, LEN, DOCS - 1), 1)
    seg_ids = jnp.sum((positions >= doc_ends[:, None, :]).astype(jnp.int32), axis=2)
    return seg_ids.reshape(2, MICRO, ROWS, LEN).astype(jnp.int32)


def draw_cross_proj(key, part):
    key = jax.random.fold_in(key, 5)
    array_shape = (2, D, 2, D)
    noise = jax.random.truncated_normal(key, -4.0, 4.0, array_shape, jnp.float32)
    section_place = lax.broadcasted_iota(jnp.int32, array_shape, 0)
    slot_place = lax.broadcasted_iota(jnp.int32, array_shape, 2)
    output_part = jnp.logical_and(section_place == 1, slot_place == 1)
    return (noise * jnp.where(output_part, 1.0 / math.sqrt(D // 128), 1.0 / math.sqrt(D))).astype(jnp.bfloat16)


def draw_norms(key, part):
    key = jax.random.fold_in(key, 7)
    array_shape = (2, 3, 2, D)
    noise = jax.random.truncated_normal(key, -3.0, 3.0, array_shape, jnp.float32)
    gain_place = lax.broadcasted_iota(jnp.int32, array_shape, 2) == 0
    return jnp.where(gain_place, 1.0 + 0.15 * noise, 0.25 * noise)


def block_scale(stream_key, extent, pieces, least, top_value):
    level, own = 1.0, jax.random.fold_in(stream_key, 6)
    for axis_at, blocks in pieces:
        draws = jnp.exp(jax.random.uniform(jax.random.fold_in(own, axis_at), (blocks,), jnp.float32, least / len(pieces), top_value / len(pieces)))
        level = level * jnp.repeat(draws, extent[axis_at] // blocks).reshape([-1 if axis == axis_at else 1 for axis in range(len(extent))])
    return level


def scatter_about(rng, shape, scale, bound, cuts=(), kind=jnp.bfloat16):
    drawn = jax.random.normal(rng, shape, jnp.float32) * scale
    if len(cuts) > 0:
        drawn = block_scale(rng, shape, cuts, -0.22, 0.18) * drawn
    return jnp.clip(drawn, min=-bound, max=bound).astype(kind)


def setup_inputs(seed: int = 0) -> dict:
    seeds = jax.random.split(jax.random.key(seed), 10)
    tokens = scatter_about(seeds[0], (2, MICRO, ROWS, LEN, D), 1.0, 6.0, ((0, 2), (3, 16)))
    segments = draw_segments(jax.random.fold_in(seeds[9], 71), 0)
    cotangent = scatter_about(seeds[2], (MICRO, ROWS, LEN, D), 1.0, 6.0, ((2, 16),))
    attn_in = scatter_about(seeds[3], (2, D, 3, D), D ** -0.5, 0.21875, ((0, 2), (3, 4)))
    attn_out = scatter_about(seeds[4], (2, D, D), (D // 128) ** -0.5, 2.5, ((0, 2), (1, 4)))
    ffn_in = scatter_about(seeds[5], (2, D, FF), D ** -0.5, 0.21875, ((0, 2), (2, 4)))
    ffn_out = scatter_about(seeds[6], (2, FF, D), FF ** -0.5, 0.109375, ((0, 2), (1, 4)))
    cross_proj = draw_cross_proj(jax.random.fold_in(seeds[9], 71), 0)
    norms = draw_norms(jax.random.fold_in(seeds[9], 71), 0)
    return dict(tokens=tokens, segments=segments, cotangent=cotangent, attn_in=attn_in, attn_out=attn_out, ffn_in=ffn_in, ffn_out=ffn_out, cross_proj=cross_proj, norms=norms)


@jax.custom_vjp
def low(v):
    return lax.optimization_barrier(v.astype(jnp.bfloat16)).astype(jnp.float32)

@jax.custom_vjp
def low_back(v):
    return v

def low_keep(v):
    return (low(v), None)

def low_pass(kept, grad):
    return (grad,)

def back_keep(v):
    return (v, None)

def back_low(kept, grad):
    return (low(grad),)
low.defvjp(low_keep, low_pass)
low_back.defvjp(back_keep, back_low)
EPSILON = 1e-05
NEGATIVE = -1e+30
HIGH = lax.Precision.HIGHEST

def norm_layer(values, gain, shift):
    center = lax.optimization_barrier(jnp.mean(values, axis=-1, keepdims=True))
    centered = values - center
    spread = lax.optimization_barrier(jnp.mean(centered * centered, axis=-1, keepdims=True))
    return centered * lax.rsqrt(spread + EPSILON) * gain + shift

def project(values, weight):
    return jnp.tensordot(values, weight, axes=1, precision=HIGH)

def attention(queries, key_rows, value_rows, allowed):
    query_len = queries.shape[0]
    key_len = key_rows.shape[0]
    head_count = queries.shape[1] // HEAD_DIM
    raw_scores = jnp.einsum('qhe,khe->hqk', queries.reshape(query_len, head_count, HEAD_DIM), key_rows.reshape(key_len, head_count, HEAD_DIM), precision=HIGH)
    scores = jnp.where(allowed[None], low_back(raw_scores) * (1.0 / math.sqrt(HEAD_DIM)), NEGATIVE)
    attn_probs = jax.nn.softmax(scores, axis=-1)
    mixed_heads = jnp.einsum('hqk,khe->qhe', low(attn_probs), value_rows.reshape(key_len, head_count, HEAD_DIM), precision=HIGH)
    return low(low_back(mixed_heads.reshape(query_len, head_count * HEAD_DIM)))

def self_attention(hidden, weight_in, weight_out, allowed):
    packed = low(low_back(project(low(hidden), weight_in)))
    mixed_heads = attention(packed[:, 0], packed[:, 1], packed[:, 2], allowed)
    return low_back(project(mixed_heads, weight_out))

def feed_forward(hidden, weight_up, weight_down):
    hidden_pre = low_back(project(low(hidden), weight_up))
    return low_back(project(low(jax.nn.gelu(hidden_pre, approximate=False)), weight_down))

def layer_pair(params, source, target, source_seg, target_seg):
    attn_in, attn_out, ffn_in, ffn_out, cross_proj, norms = params
    positions = jnp.arange(LEN)
    enc_mask = source_seg[:, None] == source_seg[None, :]
    dec_mask = jnp.logical_and(target_seg[:, None] == target_seg[None, :], positions[None, :] <= positions[:, None])
    cross_mask = target_seg[:, None] == source_seg[None, :]
    layer_entry = norm_layer(source, norms[0, 1, 0], norms[0, 1, 1])
    after_self = norm_layer(layer_entry + self_attention(layer_entry, attn_in[0], attn_out[0], enc_mask), norms[0, 0, 0], norms[0, 0, 1])
    memory = norm_layer(after_self + feed_forward(after_self, ffn_in[0], ffn_out[0]), norms[0, 2, 0], norms[0, 2, 1])
    memory_pairs = low(low_back(project(low(memory), cross_proj[0])))
    dec_first = norm_layer(target + self_attention(target, attn_in[1], attn_out[1], dec_mask), norms[1, 0, 0], norms[1, 0, 1])
    queries = low(low_back(project(low(dec_first), cross_proj[1][:, 0])))
    mixed_cross = attention(queries, memory_pairs[:, 0], memory_pairs[:, 1], cross_mask)
    crossed = low_back(jnp.einsum('qj,dj->qd', mixed_cross, cross_proj[1][:, 1], precision=HIGH))
    dec_second = norm_layer(dec_first + crossed, norms[1, 1, 0], norms[1, 1, 1])
    decoded = norm_layer(dec_second + feed_forward(dec_second, ffn_in[1], ffn_out[1]), norms[1, 2, 0], norms[1, 2, 1])
    return (memory, decoded)

def reference(tokens, segments, cotangent, attn_in, attn_out, ffn_in, ffn_out, cross_proj, norms):
    params = (attn_in.astype(jnp.float32), attn_out.astype(jnp.float32), ffn_in.astype(jnp.float32), ffn_out.astype(jnp.float32), cross_proj.astype(jnp.float32), norms.astype(jnp.float32))
    row_total = MICRO * ROWS
    sources = tokens[0].reshape(row_total, LEN, D).astype(jnp.float32)
    targets = tokens[1].reshape(row_total, LEN, D).astype(jnp.float32)
    source_segs = segments[0].reshape(row_total, LEN)
    target_segs = segments[1].reshape(row_total, LEN)
    cotangents = cotangent.reshape(row_total, LEN, D).astype(jnp.float32)

    def one_row(totals, row_data):
        source, target, source_seg, target_seg, row_cot = row_data

        def run_pair(param_set, source_in, target_in):
            return layer_pair(param_set, source_in, target_in, source_seg, target_seg)
        (memory, decoded), pull_back = jax.vjp(run_pair, params, source, target)
        grad_params, grad_source, grad_target = pull_back((jnp.zeros_like(memory), row_cot))
        totals = jax.tree.map(jnp.add, totals, grad_params)
        return (totals, (memory.astype(jnp.bfloat16), decoded.astype(jnp.bfloat16), grad_source, grad_target))
    zero_totals = jax.tree.map(jnp.zeros_like, params)
    totals, (memories, decodes, grad_sources, grad_targets) = lax.scan(one_row, zero_totals, (sources, targets, source_segs, target_segs, cotangents))
    outputs = jnp.stack([memories, decodes]).reshape(2, MICRO, ROWS, LEN, D)
    token_grads = jnp.stack([grad_sources, grad_targets]).reshape(2, MICRO, ROWS, LEN, D)
    return (outputs, token_grads, totals[0], totals[1], totals[2], totals[3], totals[4], totals[5])
```

```python
import functools
import math

import jax
import jax.numpy as jnp
from jax import lax
from jax.experimental import pallas as pl
from jax.experimental.pallas import tpu as pltpu
from jax.sharding import Mesh, PartitionSpec as P

EPSILON = 1e-05
NEGATIVE = -1e30
BF = jnp.bfloat16
F32 = jnp.float32
I32 = jnp.int32
ROOT_HALF = 1.0 / math.sqrt(2.0)
DENSITY = 1.0 / math.sqrt(2.0 * math.pi)
VMEM = pl.BlockSpec(memory_space=pltpu.VMEM)
SMEM = pl.BlockSpec(memory_space=pltpu.SMEM)
ANY = pl.BlockSpec(memory_space=pl.ANY)


def shift(value, axis, steps):
    count = lax.axis_size(axis)
    return lax.ppermute(value, axis, [(i, (i + steps) % count) for i in range(count)])


def swap_core(value):
    return shift(value, "core", 1)


def section_pairs(own, other, flip):
    return [(own * 2 + i, other * 2 + (i ^ flip)) for i in range(2)]


def gather_z(rows):
    return [rows] + [shift(rows, "tensor", -j) for j in range(1, 4)]


def scatter_z(chunks):
    return [chunks[0]] + [shift(chunks[j], "tensor", j) for j in range(1, 4)]


def mm(a, b):
    return jnp.dot(a, b, preferred_element_type=F32)


def mm_nt(a, b):
    return lax.dot_general(a, b, (((1,), (1,)), ((), ())), preferred_element_type=F32)


def mm_tn(a, b):
    return lax.dot_general(a, b, (((0,), (0,)), ((), ())), preferred_element_type=F32)


def erf(v):
    v = jnp.clip(v, -4.0, 4.0)
    w = v * v
    top = -2.72614225801306e-10
    for c in (2.77068142495902e-08, -2.10102402082508e-06, -5.69250639462346e-05, -7.34990630326855e-04,
              -2.95459980854025e-03, -1.60960333262415e-02):
        top = top * w + c
    low = -1.45660718464996e-05
    for c in (-2.13374055278905e-04, -1.68282697438203e-03, -7.37332916720468e-03, -1.42647390514189e-02):
        low = low * w + c
    return v * top / low


def gelu(v):
    return v * (0.5 + 0.5 * erf(v * ROOT_HALF))


def gelu_slope(v):
    return 0.5 + 0.5 * erf(v * ROOT_HALF) + v * (jnp.exp(-0.5 * v * v) * DENSITY)


def normed(values):
    centered = values - jnp.mean(values, axis=-1, keepdims=True)
    inv = lax.rsqrt(jnp.mean(centered * centered, axis=-1, keepdims=True) + EPSILON)
    return centered * inv, inv


def norm_forward(values, gain, bias):
    return normed(values)[0] * gain + bias


def norm_backward(grad, values, gain):
    unit, inv = normed(values)
    scaled = grad * gain
    inner = jnp.mean(scaled * unit, axis=-1, keepdims=True)
    back = inv * (scaled - jnp.mean(scaled, axis=-1, keepdims=True) - unit * inner)
    sums = jnp.concatenate([jnp.sum(grad * unit, axis=0, keepdims=True), jnp.sum(grad, axis=0, keepdims=True)], axis=0)
    return back, sums


def pick(flag, one, zero):
    return jnp.where(jnp.full(one.shape, flag, I32) == 1, one, zero)


def call(kernel, outs, *args, scalars=(), after=(), scratch=(), **kw):
    shapes = [jax.ShapeDtypeStruct(s, d) for s, d in outs]
    count = len(scalars) + len(args)

    def body(*refs):
        kernel(*refs[:count], *refs[count + len(after) :], **kw)

    return pl.pallas_call(
        body,
        out_shape=shapes,
        in_specs=[SMEM] * len(scalars) + [VMEM] * len(args) + [ANY] * len(after),
        out_specs=[VMEM] * len(outs),
        scratch_shapes=[pltpu.VMEM(s, d) for s, d in scratch],
        compiler_params=pltpu.CompilerParams(vmem_limit_bytes=20 * 1024 * 1024),
        cost_estimate=pl.CostEstimate(flops=1, bytes_accessed=1, transcendentals=0),
        name=kernel.__name__,
    )(*scalars, *args, *after)


ROWS_F = ((64, 768), F32)
ROWS_B = ((64, 768), BF)
PAIR_F = ((2, 768), F32)
BOTH_B = ((128, 768), BF)
CHUNKS = [ROWS_F, ROWS_B, ROWS_B, ROWS_B]


def put_chunks(partial, refs):
    for j, ref in enumerate(refs):
        ref[...] = partial[64 * j : 64 * j + 64].astype(ref.dtype)


def add_chunks(refs):
    total = refs[0][...]
    for ref in refs[1:]:
        total = total + ref[...].astype(F32)
    return total


def all_rows(refs, part=None):
    cut = slice(None) if part is None else slice(64 * part, 64 * part + 64)
    return jnp.concatenate([ref[cut] for ref in refs], axis=0)


def entry_kernel(at, arrived, norm, w_in, low, own, queries, kv):
    dec, z = at[0], at[4]
    for j in range(4):
        rows = arrived[lax.rem(z + j, 4)].astype(F32)
        rows = pick(dec, rows, norm_forward(rows, norm[1, 0:1], norm[1, 1:2]))
        low[64 * j : 64 * j + 64] = rows.astype(BF)
        if j == 0:
            own[...] = rows
    packed = mm(low[...], w_in[...])
    queries[...] = packed[:, :192].astype(BF)
    kv[...] = packed[:, 192:].astype(BF)


def cell_places(at, index, other_x, other_c):
    x, c, z = at[1] ^ other_x, at[3] ^ other_c, at[4]
    block = (x * 4 + ((index // 64 + z) & 3)) * 2 + c
    return block * 64 + (index & 63)


def documents(place, ends, slot):
    return sum((place >= ends[slot, d]).astype(I32) for d in range(3))


def score_bias(at, ends, query_slot, key_slot, causal):
    q_place = cell_places(at, lax.broadcasted_iota(I32, (1, 256), 1), 0, 0)
    q_doc = documents(q_place, ends, query_slot)
    out = []
    for chunk in range(4):
        k_place = cell_places(at, lax.broadcasted_iota(I32, (256, 1), 0), chunk // 2, chunk % 2)
        k_doc = documents(k_place, ends, key_slot)
        bias = jnp.where(k_doc == q_doc, 0.0, NEGATIVE)
        if causal:
            bias = jnp.where(k_place - q_place > (1 - at[0]) * 2048, NEGATIVE, bias)
        out.append(bias)
    return out


def attend_kernel(at, ends, queries, kv0, kv1, kv2, kv3, w_out, mixed, *chunks, cross):
    slot = (1, 0) if cross else (at[0], at[0])
    bias = score_bias(at, ends, slot[0], slot[1], not cross)
    kvs = (kv0, kv1, kv2, kv3)
    heads = []
    for h in range(3):
        cols = slice(64 * h, 64 * h + 64)
        vals = slice(192 + 64 * h, 256 + 64 * h)
        q = queries[:, cols]
        scores = [mm_nt(kv[:, cols], q) * 0.125 + b for kv, b in zip(kvs, bias)]
        top = functools.reduce(jnp.maximum, [jnp.max(s, axis=0, keepdims=True) for s in scores])
        weights = [jnp.exp(s - top) for s in scores]
        total = sum(jnp.sum(w, axis=0, keepdims=True) for w in weights)
        inv = 1.0 / total
        out = sum(mm_tn(kv[:, vals], (w * inv).astype(BF)) for kv, w in zip(kvs, weights))
        heads.append(out.T)
    joined = jnp.concatenate(heads, axis=1).astype(BF)
    mixed[...] = joined
    put_chunks(mm_nt(joined, w_out[...]) if cross else mm(joined, w_out[...]), chunks)


def attend_back_kernel(at, ends, g0, g1, g2, g3, queries, kv0, kv1, kv2, kv3, w_out, grad_q, keep, send, *, cross):
    slot = (1, 0) if cross else (at[0], at[0])
    bias = score_bias(at, ends, slot[0], slot[1], not cross)
    kvs = (kv0, kv1, kv2, kv3)
    rows = all_rows((g0, g1, g2, g3))
    grad_mixed = (mm(rows, w_out[...]) if cross else mm_nt(rows, w_out[...])).astype(BF)
    grads = []
    for h in range(3):
        cols = slice(64 * h, 64 * h + 64)
        vals = slice(192 + 64 * h, 256 + 64 * h)
        q = queries[:, cols]
        g = grad_mixed[:, cols]
        scores = [mm_nt(kv[:, cols], q) * 0.125 + b for kv, b in zip(kvs, bias)]
        top = functools.reduce(jnp.maximum, [jnp.max(s, axis=0, keepdims=True) for s in scores])
        weights = [jnp.exp(s - top) for s in scores]
        inv = 1.0 / sum(jnp.sum(w, axis=0, keepdims=True) for w in weights)
        probs = [w * inv for w in weights]
        grad_probs = [mm_nt(kv[:, vals], g) for kv in kvs]
        inner = sum(jnp.sum(p * d, axis=0, keepdims=True) for p, d in zip(probs, grad_probs))
        raw = [(p * (d - inner) * 0.125).astype(BF) for p, d in zip(probs, grad_probs)]
        for chunk in range(4):
            ref = keep if chunk % 2 == 0 else send
            ref[chunk // 2, :, cols] = mm(raw[chunk], q).astype(ref.dtype)
            ref[chunk // 2, :, vals] = mm(probs[chunk].astype(BF), g).astype(ref.dtype)
        grads.append(sum(mm_tn(kv[:, cols], r) for kv, r in zip(kvs, raw)).T)
    grad_q[...] = jnp.concatenate(grads, axis=1).astype(BF)


def halves_kernel(at, w_up, w_down, up, down):
    @pl.when(at[3] == 0)
    def _():
        up[...] = w_up[:, :384].T
        down[...] = w_down[:384]

    @pl.when(at[3] == 1)
    def _():
        up[...] = w_up[:, 384:].T
        down[...] = w_down[384:]


def add_norm_kernel(base, r0, r1, r2, r3, norm, sums, after, low, *, index):
    values = base[...] + add_chunks((r0, r1, r2, r3))
    sums[...] = values
    out = norm_forward(values, norm[index, 0:1], norm[index, 1:2])
    after[...] = out
    low[...] = out.astype(BF)


def memory_kernel(base, keep, got, norm, first, sums, low, both):
    values = base[...] + keep[...] + got[...].astype(F32)
    sums[...] = values
    out = norm_forward(values, norm[2, 0:1], norm[2, 1:2]).astype(BF)
    low[...] = out
    both[0:64] = out
    both[64:128] = first[...]


def pairs_kernel(a0, a1, a2, a3, w_cross, out):
    out[...] = mm(all_rows((a0, a1, a2, a3), 0), w_cross[...]).astype(BF)


def query_kernel(a0, a1, a2, a3, w_cross, out):
    out[...] = mm(all_rows((a0, a1, a2, a3), 1), w_cross[:, :192]).astype(BF)


def ffn_kernel(own, other, u0, u1, u2, u3, d0, d1, d2, d3, keep, send):
    rows = all_rows((own, other))
    total = 0.0
    for up, down in ((u0, d0), (u1, d1), (u3, d3), (u2, d2)):
        total = total + mm(gelu(mm_nt(rows, up[...])).astype(BF), down[...])
    keep[...] = total[:64]
    send[...] = total[64:].astype(BF)


def ffn_back_kernel(own, other, g_own, g_other, u0, u1, u2, u3, d0, d1, d2, d3, keep, send):
    rows = all_rows((own, other))
    grad = all_rows((g_own, g_other))
    total = 0.0
    for up, down in ((u0, d0), (u1, d1), (u3, d3), (u2, d2)):
        slope = gelu_slope(mm_nt(rows, up[...]))
        total = total + mm((mm_nt(grad, down[...]) * slope).astype(BF), up[...])
    keep[...] = total[:64]
    send[...] = total[64:].astype(BF)


def turn_kernel(base, keep, got, cot, norm, decoded, grad, low, pair):
    values = base[...] + keep[...] + got[...].astype(F32)
    unit, inv = normed(values)
    gain = norm[2, 0:1]
    decoded[...] = (unit * gain + norm[2, 1:2]).astype(BF)
    up = cot[...].astype(F32)
    scaled = up * gain
    inner = jnp.mean(scaled * unit, axis=-1, keepdims=True)
    back = inv * (scaled - jnp.mean(scaled, axis=-1, keepdims=True) - unit * inner)
    grad[...] = back
    low[...] = back.astype(BF)
    pair[...] = jnp.concatenate([jnp.sum(up * unit, axis=0, keepdims=True), jnp.sum(up, axis=0, keepdims=True)], axis=0)


def ffn_norm_back_kernel(base, keep, got, values, norm, grad, low, pair):
    up = base[...] + keep[...] + got[...].astype(F32)
    back, sums = norm_backward(up, values[...], norm[1, 0:1])
    grad[...] = back
    low[...] = back.astype(BF)
    pair[...] = sums


def add_core_kernel(keep, got, out):
    out[...] = (keep[...] + got[...].astype(F32)).astype(BF)


def add_core_self_kernel(keep, got, own, send):
    total = keep[...] + got[...].astype(F32)
    own[...] = total[0]
    send[...] = total[1].astype(BF)


def project_back_kernel(at, m0, m1, grad_q, w_cross, grad_pairs, *chunks):
    total = (m0[...].astype(F32) + m1[...].astype(F32)).astype(BF)
    grad_pairs[...] = total
    mine = jnp.concatenate([grad_q[...], jnp.zeros((256, 192), BF)], axis=1)
    mine = pick(at[0], mine.astype(F32), total.astype(F32)).astype(BF)
    put_chunks(mm_nt(mine, w_cross[...]), chunks)


def memory_back_kernel(at, r0, r1, r2, r3, values, norm, in_d, in_e, grad_d, total, grad, low, pair, both):
    up = add_chunks((r0, r1, r2, r3))
    total[...] = up
    back, sums = norm_backward(up, values[...], norm[2, 0:1])
    grad[...] = back
    low[...] = back.astype(BF)
    pair[...] = sums
    both[0:64] = pick(at[0], in_d[...].astype(F32), in_e[...].astype(F32)).astype(BF)
    both[64:128] = pick(at[0], grad_d[...].astype(F32), back).astype(BF)


def first_norm_back_kernel(at, grad_e, keep, got, grad_d, low_sum, values, norm, grad, low, pair):
    enc = grad_e[...] + keep[...] + got[...].astype(F32)
    up = pick(at[0], grad_d[...] + low_sum[...], enc)
    back, sums = norm_backward(up, values[...], norm[0, 0:1])
    grad[...] = back
    low[...] = back.astype(BF)
    pair[...] = sums


def entry_back_kernel(grad_q, own, got, w_in, packed, *chunks):
    kv = (own[...] + got[...].astype(F32)).astype(BF)
    packed[...] = jnp.concatenate([grad_q[...], kv], axis=1)
    put_chunks(mm_nt(packed[...], w_in[...]), chunks)


def last_norm_back_kernel(at, base, r0, r1, r2, r3, tokens, norm, n0, n1, n2_d, n2_e, out):
    up = base[...] + add_chunks((r0, r1, r2, r3))
    back, sums = norm_backward(up, tokens[...].astype(F32), norm[1, 0:1])
    out[0:64] = pick(at[0], up, back).astype(BF)
    pairs = jnp.concatenate([n0[...], pick(at[0], n1[...], sums), pick(at[0], n2_d[...], n2_e[...]), jnp.zeros((2, 768), F32)], axis=0)
    out[64:80] = two_parts(pairs)


def two_parts(values):
    high = values.astype(BF).astype(F32)
    return jnp.concatenate([high, values - high], axis=0).astype(BF)


def one_part(rows):
    rows = rows.astype(F32)
    return rows[:8] + rows[8:]


def collect_kernel(at, p0, p1, p2, p3, grads, sums):
    parts = jnp.zeros((4, 8, 768), F32)
    place = lax.broadcasted_iota(I32, (4, 8, 768), 0)
    for k, ref in enumerate((p0, p1, p2, p3)):
        micro = (at[4] - k) & 3
        grads[micro] = ref[0:64].astype(F32)
        parts = jnp.where(place == micro, one_part(ref[64:80])[None], parts)
    sums[...] = (parts[0] + parts[1]) + (parts[2] + parts[3])


def outputs_kernel(at, p0, p1, p2, p3, out):
    for k, ref in enumerate((p0, p1, p2, p3)):
        out[(at[4] - k) & 3] = ref[...]


def split_core(full, at, keep, send):
    half = keep.shape[0]
    keep[...] = full[pl.ds(pl.multiple_of(at[3] * half, 16), half)]
    send[...] = full[pl.ds(pl.multiple_of((1 - at[3]) * half, 16), half)]


def ffn_weights_kernel(at, *refs):
    both, memory, crossed = (refs[4 * i : 4 * i + 4] for i in range(3))
    grad_pairs, grad_q, mixed, w_up, w_down, keep, send, full = refs[12:]
    flag = at[0]

    def choose(one, zero):
        return pick(flag, one.astype(F32), zero.astype(F32)).astype(BF)

    rows = all_rows(both, 0)
    grad = all_rows(both, 1)
    pre = mm(rows, w_up[...])
    grad_pre = (mm_nt(grad, w_down[...]) * gelu_slope(pre)).astype(BF)
    full[0:768] = mm_tn(rows, grad_pre).astype(BF)
    full[768:1536] = mm_tn(gelu(pre).astype(BF), grad).astype(BF)
    memories = all_rows(memory, 0)
    left = mm_tn(choose(all_rows(memory, 1), memories), choose(grad_q[...], grad_pairs[:, :192])).astype(BF)
    right = mm_tn(choose(all_rows(crossed), memories), choose(mixed[...], grad_pairs[:, 192:])).astype(BF)
    cross = jnp.concatenate([left, right], axis=1)
    full[1536:1920] = jnp.concatenate([cross[:384], cross[384:]], axis=1)
    split_core(full, at, keep, send)


def attn_weights_kernel(at, low, packed, mixed, g0, g1, g2, g3, keep, send, full):
    grad_in = mm_tn(low[...], packed[...]).astype(BF)
    grad_out = mm_tn(all_rows((g0, g1, g2, g3)), mixed[...]).astype(BF)
    full[...] = jnp.concatenate([grad_in, grad_out], axis=1)
    split_core(full, at, keep, send)


def split_y_kernel(at, keep, got, own, s1, s2, s3, full):
    full[...] = (keep[...].astype(F32) + got[...].astype(F32)).astype(BF)
    rows = own.shape[0]
    for j, ref in enumerate((own, s1, s2, s3)):
        ref[...] = full[pl.ds(pl.multiple_of(((at[2] + j) & 3) * rows, 16), rows)]


def add_all_kernel(*refs):
    total = refs[0][...].astype(F32)
    for ref in refs[1:-1]:
        total = total + ref[...].astype(F32)
    refs[-1][...] = total.astype(refs[-1].dtype)


def join_y_kernel(at, t0, t1, t2, t3, half):
    rows = t0.shape[0]
    for j, ref in enumerate((t0, t1, t2, t3)):
        half[pl.ds(pl.multiple_of(((at[2] + j) & 3) * rows, 16), rows)] = ref[...]


def pack_norms_kernel(own, got, sums, xh_sums, out):
    rows = own.shape[0]
    out[0:rows] = (own[...].astype(F32) + got[...].astype(F32)).astype(BF)
    out[rows : rows + 16] = two_parts(sums[...] + xh_sums[...])


def join_norms_kernel(at, t0, t1, t2, t3, half, norms):
    rows = t0.shape[0] - 16
    parts = jnp.zeros((4, 8, 768), F32)
    place = lax.broadcasted_iota(I32, (4, 8, 768), 0)
    for j, ref in enumerate((t0, t1, t2, t3)):
        y = (at[2] + j) & 3
        half[pl.ds(pl.multiple_of(y * rows, 16), rows)] = ref[0:rows]
        parts = jnp.where(place == y, one_part(ref[rows : rows + 16])[None], parts)
    norms[...] = (parts[0] + parts[1]) + (parts[2] + parts[3])


def join_core(at, own, got, full):
    half = own.shape[0]
    full[pl.ds(pl.multiple_of(at[3] * half, 16), half)] = own[...]
    full[pl.ds(pl.multiple_of((1 - at[3]) * half, 16), half)] = got[...]


def ffn_final_kernel(at, own, got, up, down, cross, full):
    join_core(at, own, got, full)
    up[...] = full[0:768].astype(F32)
    down[...] = full[768:1536].astype(F32)
    cross[0:384] = full[1536:1920, :384].astype(F32)
    cross[384:768] = full[1536:1920, 384:].astype(F32)


def attn_final_kernel(at, own, got, grad_in, grad_out, full):
    join_core(at, own, got, full)
    grad_in[...] = full[:, :576].astype(F32)
    grad_out[...] = full[:, 576:].astype(F32).T


def reduce_y(at, keep, got, after=()):
    rows, cols = keep.shape
    own, *sends = call(
        split_y_kernel, [((rows // 4, cols), BF)] * 4, keep, got, scalars=(at,), after=after, scratch=[((rows, cols), BF)]
    )
    return [own] + [shift(s, "y", j + 1) for j, s in enumerate(sends)]


def add_parts(parts, after=()):
    return call(add_all_kernel, [(parts[0].shape, BF)], *parts, after=after)[0]


def add_sums(one, two):
    return call(add_all_kernel, [((8, 768), F32)], one, two)[0]


def gather_y(at, total, after=()):
    parts = [total] + [shift(total, "y", -j) for j in range(1, 4)]
    rows, cols = total.shape
    return call(join_y_kernel, [((rows * 4, cols), BF)], *parts, scalars=(at,), after=after)[0]


def per_device(tokens, segments, cotangent, attn_in, attn_out, ffn_in, ffn_out, cross_proj, norms):
    w_in = attn_in[0].reshape(768, 576)
    w_out = attn_out[0]
    w_up = ffn_in[0]
    w_down = ffn_out[0]
    w_cross = cross_proj[0].reshape(768, 384)
    w_cross_out = w_cross[:, 192:]
    norm = norms[0]
    sec = lax.axis_index("section")
    x_at = lax.axis_index("xh")
    y_at = lax.axis_index("y")
    c_at = lax.axis_index("core")
    z_at = lax.axis_index("tensor")
    dec = sec == 1
    at = jnp.stack([sec, x_at, y_at, c_at, z_at]).astype(I32)

    tok = tokens[0, :, 0]
    arrived = lax.all_to_all(tok, "y", 0, 0)
    seg_micro = lax.dynamic_index_in_dim(segments[:, :, 0], y_at, 1, keepdims=False)
    ends = jnp.sum((seg_micro[:, None, :] <= jnp.arange(3, dtype=I32)[None, :, None]).astype(I32), axis=2)

    part = ((384, 768), BF)
    up_half, down_half = call(halves_kernel, [part, part], w_up, w_down, scalars=(at,))
    up_3, up_1 = shift(up_half, "tensor", 1), shift(up_half, "tensor", -1)
    down_3, down_1 = shift(down_half, "tensor", 1), shift(down_half, "tensor", -1)

    entry_low, entry_own, queries, kv = call(
        entry_kernel,
        [((256, 768), BF), ROWS_F, ((256, 192), BF), ((256, 384), BF)],
        arrived,
        norm,
        w_in,
        scalars=(at,),
        after=(up_half,),
    )
    kv_x = shift(kv, "xh", 1)
    self_kv = (kv, swap_core(kv), kv_x, swap_core(kv_x))
    cot_pairs = [(a * 4 + b, b * 4 + a) for a in range(4) for b in range(4)]
    cot_send = lax.dynamic_index_in_dim(cotangent[:, 0], z_at, 0, keepdims=False)
    cot_own = lax.ppermute(lax.optimization_barrier((cot_send, kv_x))[0], ("y", "tensor"), cot_pairs)
    mixed, *chunks = call(
        attend_kernel, [((256, 192), BF)] + CHUNKS, queries, *self_kv, w_out, scalars=(at, ends), cross=False
    )
    sums0, after_self, after_self_low = call(
        add_norm_kernel, [ROWS_F, ROWS_F, ROWS_B], entry_own, *scatter_z(chunks), norm, index=0
    )
    up_3_late, down_1_late, _ = lax.optimization_barrier((up_3, down_1, chunks[1]))
    ups = (up_half, up_1, shift(up_3_late, "tensor", 1), up_3)
    downs = (down_half, down_1, shift(down_1_late, "tensor", -1), down_3)

    after_self_other = swap_core(after_self_low)
    keep, send = call(ffn_kernel, [ROWS_F, ROWS_B], after_self_low, after_self_other, *ups, *downs)
    sums2, memory_low, both = call(
        memory_kernel, [ROWS_F, ROWS_B, BOTH_B], after_self, keep, swap_core(send), norm, after_self_low
    )
    memory_all = gather_z(both)
    (pairs,) = call(pairs_kernel, [((256, 384), BF)], *memory_all, w_cross)
    m0 = lax.ppermute(pairs, ("section", "xh"), section_pairs(0, 1, 0))
    m1 = lax.ppermute(pairs, ("section", "xh"), section_pairs(0, 1, 1))
    memory_kv = (m0, swap_core(m0), m1, swap_core(m1))
    (cross_q,) = call(query_kernel, [((256, 192), BF)], *memory_all, w_cross, after=(pairs,))

    mixed_cross, *chunks = call(
        attend_kernel, [((256, 192), BF)] + CHUNKS, cross_q, *memory_kv, w_cross_out, scalars=(at, ends), cross=True
    )
    sums1, after_cross, after_cross_low = call(
        add_norm_kernel, [ROWS_F, ROWS_F, ROWS_B], after_self, *scatter_z(chunks), norm, index=1
    )
    after_cross_other = swap_core(after_cross_low)
    keep, send = call(ffn_kernel, [ROWS_F, ROWS_B], after_cross_low, after_cross_other, *ups, *downs)
    decoded, grad_d2, grad_ffn_d, norm2_d = call(
        turn_kernel, [ROWS_B, ROWS_F, ROWS_B, PAIR_F], after_cross, keep, swap_core(send), cot_own, norm
    )

    keep, send = call(
        ffn_back_kernel,
        [ROWS_F, ROWS_B],
        after_cross_low,
        after_cross_other,
        grad_ffn_d,
        swap_core(grad_ffn_d),
        *ups,
        *downs,
    )
    grad_d1, grad_d1_low, norm1_d = call(
        ffn_norm_back_kernel, [ROWS_F, ROWS_B, PAIR_F], grad_d2, keep, swap_core(send), sums1, norm
    )
    grad_crossed_all = gather_z(grad_d1_low)
    back_shapes = [((256, 192), BF), ((2, 256, 384), F32), ((2, 256, 384), BF)]
    grad_q_cross, keep, send = call(
        attend_back_kernel,
        back_shapes,
        *grad_crossed_all,
        cross_q,
        *memory_kv,
        w_cross_out,
        scalars=(at, ends),
        cross=True,
    )
    (grad_mkv,) = call(add_core_kernel, [((2, 256, 384), BF)], keep, swap_core(send))
    g0 = lax.ppermute(grad_mkv[0], ("section", "xh"), section_pairs(1, 0, 0))
    g1 = lax.ppermute(grad_mkv[1], ("section", "xh"), section_pairs(1, 0, 1))


    def spread(rows):
        parts = []
        for k in range(4):
            pairs = [(m * 4 + b, b * 4 + (m + k) % 4) for m in range(4) for b in range(4)]
            parts.append(lax.ppermute(rows, ("y", "tensor"), pairs))
        return parts

    out_low = jnp.where(dec, decoded, memory_low)
    out_parts = spread(lax.optimization_barrier((out_low, grad_mkv))[0])

    grad_pairs, *chunks = call(
        project_back_kernel, [((256, 384), BF)] + CHUNKS, g0, g1, grad_q_cross, w_cross, scalars=(at,)
    )
    low_sum, grad_e2, grad_ffn_e, norm2_e, both = call(
        memory_back_kernel,
        [ROWS_F, ROWS_F, ROWS_B, PAIR_F, BOTH_B],
        *scatter_z(chunks),
        sums2,
        norm,
        after_cross_low,
        after_self_low,
        grad_ffn_d,
        scalars=(at,),
        after=out_parts,
    )
    keep, send = call(
        ffn_back_kernel,
        [ROWS_F, ROWS_B],
        after_self_low,
        after_self_other,
        grad_ffn_e,
        swap_core(grad_ffn_e),
        *ups,
        *downs,
    )
    both_all = gather_z(both)
    grad_0, grad_0_low, norm0 = call(
        first_norm_back_kernel,
        [ROWS_F, ROWS_B, PAIR_F],
        grad_e2,
        keep,
        swap_core(send),
        grad_d1,
        low_sum,
        sums0,
        norm,
        scalars=(at,),
    )
    grad_sa_all = gather_z(grad_0_low)
    (outputs,) = call(outputs_kernel, [((4, 64, 768), BF)], *out_parts, scalars=(at,), after=(grad_0_low,))

    half = ((960, 768), BF)
    w_keep, w_send = call(
        ffn_weights_kernel,
        [half, half],
        *both_all,
        *memory_all,
        *grad_crossed_all,
        grad_pairs,
        grad_q_cross,
        mixed_cross,
        w_up,
        w_down,
        scalars=(at,),
        scratch=[((1920, 768), BF)],
        after=(grad_sa_all[2],),
    )
    w_got = swap_core(w_send)

    grad_q, keep, send = call(
        attend_back_kernel,
        back_shapes,
        *grad_sa_all,
        queries,
        *self_kv,
        w_out,
        scalars=(at, ends),
        after=(w_keep,),
        cross=False,
    )
    w_parts = reduce_y(at, w_keep, w_got, after=(grad_q,))
    own_kv, send_kv = call(
        add_core_self_kernel, [((256, 384), F32), ((256, 384), BF)], keep, swap_core(send)
    )
    grad_packed, *chunks = call(
        entry_back_kernel,
        [((256, 576), BF)] + CHUNKS,
        grad_q,
        own_kv,
        shift(send_kv, "xh", 1),
        w_in,
        after=(w_parts[0],),
    )
    tok_own = lax.dynamic_index_in_dim(arrived, z_at, 0, keepdims=False)
    got_chunks = scatter_z(chunks)
    half = ((384, 768), BF)
    a_keep, a_send = call(
        attn_weights_kernel,
        [half, half],
        entry_low,
        grad_packed,
        mixed,
        *grad_sa_all,
        scalars=(at,),
        scratch=[((768, 768), BF)],
        after=(got_chunks[2],),
    )
    a_parts = reduce_y(at, a_keep, swap_core(a_send))
    (grad_own,) = call(
        last_norm_back_kernel,
        [((80, 768), BF)],
        grad_0,
        *got_chunks,
        tok_own,
        norm,
        norm0,
        norm1_d,
        norm2_d,
        norm2_e,
        scalars=(at,),
        after=(a_parts[0],),
    )
    tok_parts = spread(grad_own)
    w_piece = add_parts(w_parts, after=(grad_own,))
    w_got = shift(w_piece, "xh", 1)
    a_piece = add_parts(a_parts, after=(w_piece,))
    a_got = shift(a_piece, "xh", 1)
    token_grads, sums = call(
        collect_kernel, [((4, 64, 768), F32), ((8, 768), F32)], *tok_parts, scalars=(at,), after=(a_piece,)
    )
    sums = add_sums(sums, swap_core(sums))
    w_total = add_parts([w_piece, w_got], after=(sums,))
    xh_sums = shift(sums, "xh", 1)
    (a_total,) = call(pack_norms_kernel, [((112, 768), BF)], a_piece, a_got, sums, xh_sums)
    a_half, norm_sums = call(
        join_norms_kernel,
        [((384, 768), BF), ((8, 768), F32)],
        *([a_total] + [shift(a_total, "y", -j) for j in range(1, 4)]),
        scalars=(at,),
    )
    w_half = gather_y(at, w_total)
    grad_in, grad_out = call(
        attn_final_kernel,
        [((768, 576), F32), ((192, 768), F32)],
        a_half,
        swap_core(a_half),
        scalars=(at,),
        scratch=[((768, 768), BF)],
    )
    grad_up, grad_down, grad_cross = call(
        ffn_final_kernel,
        [((768, 768), F32), ((768, 768), F32), ((768, 384), F32)],
        w_half,
        swap_core(w_half),
        scalars=(at,),
        scratch=[((1920, 768), BF)],
    )
    return (
        outputs[None, :, None],
        token_grads[None, :, None],
        grad_in.reshape(1, 768, 3, 192),
        grad_out[None],
        grad_up[None],
        grad_down[None],
        grad_cross.reshape(1, 768, 2, 192),
        norm_sums[:6].reshape(1, 3, 2, 768),
    )


def solution(mesh):
    fine = Mesh(mesh.devices.reshape(2, 2, 4, 2, 4), ("section", "xh", "y", "core", "tensor"))
    dp = ("xh", "y", "core")
    weights = (
        P("section", None, None, "tensor"),
        P("section", "tensor", None),
        P("section", None, "tensor"),
        P("section", "tensor", None),
        P("section", None, None, "tensor"),
        P("section", None, None, None),
    )
    rows = P("section", None, None, dp, None)
    return jax.shard_map(
        per_device,
        mesh=fine,
        in_specs=(rows, P(), P(None, None, dp, None)) + weights,
        out_specs=(rows, rows) + weights,
        check_vma=False,
    )
```

```python
import functools
import math

import jax
import jax.numpy as jnp
from jax import lax
from jax.experimental import pallas as pl
from jax.experimental.pallas import tpu as pltpu
from jax.sharding import Mesh, PartitionSpec as P

EPSILON = 1e-05
NEGATIVE = -1e30
BF = jnp.bfloat16
F32 = jnp.float32
I32 = jnp.int32
ROOT_HALF = 1.0 / math.sqrt(2.0)
DENSITY = 1.0 / math.sqrt(2.0 * math.pi)
VMEM = pl.BlockSpec(memory_space=pltpu.VMEM)
SMEM = pl.BlockSpec(memory_space=pltpu.SMEM)
ANY = pl.BlockSpec(memory_space=pl.ANY)
HBM = pl.BlockSpec(memory_space=pltpu.HBM)
COST = pl.CostEstimate(flops=2_000_000_000, bytes_accessed=0, transcendentals=0)
LONG = pl.CostEstimate(flops=8_000_000_000, bytes_accessed=0, transcendentals=0)
LIGHT = pl.CostEstimate(flops=1000, bytes_accessed=0, transcendentals=0)


def shift(value, axis, steps):
    count = lax.axis_size(axis)
    return lax.ppermute(value, axis, [(i, (i + steps) % count) for i in range(count)])


def swap_core(value):
    return shift(value, "core", 1)


def section_pairs(own, other, flip):
    return [(own * 2 + i, other * 2 + (i ^ flip)) for i in range(2)]


def gather_z(rows):
    return [rows] + [shift(rows, "tensor", -j) for j in range(1, 4)]


def scatter_z(chunks):
    return [chunks[0]] + [shift(chunks[j], "tensor", j) for j in range(1, 4)]


def mm(a, b):
    return jnp.dot(a, b, preferred_element_type=F32)


def mm_nt(a, b):
    return lax.dot_general(a, b, (((1,), (1,)), ((), ())), preferred_element_type=F32)


def mm_tn(a, b):
    return lax.dot_general(a, b, (((0,), (0,)), ((), ())), preferred_element_type=F32)


def erf(v):
    v = jnp.clip(v, -4.0, 4.0)
    w = v * v
    top = -2.72614225801306e-10
    for c in (2.77068142495902e-08, -2.10102402082508e-06, -5.69250639462346e-05, -7.34990630326855e-04,
              -2.95459980854025e-03, -1.60960333262415e-02):
        top = top * w + c
    low = -1.45660718464996e-05
    for c in (-2.13374055278905e-04, -1.68282697438203e-03, -7.37332916720468e-03, -1.42647390514189e-02):
        low = low * w + c
    return v * top / low


def gelu(v):
    return v * (0.5 + 0.5 * erf(v * ROOT_HALF))


def gelu_slope(v):
    return 0.5 + 0.5 * erf(v * ROOT_HALF) + v * (jnp.exp(-0.5 * v * v) * DENSITY)


def normed(values):
    centered = values - jnp.mean(values, axis=-1, keepdims=True)
    inv = lax.rsqrt(jnp.mean(centered * centered, axis=-1, keepdims=True) + EPSILON)
    return centered * inv, inv


def norm_forward(values, gain, bias):
    return normed(values)[0] * gain + bias


def norm_backward(grad, values, gain):
    unit, inv = normed(values)
    scaled = grad * gain
    inner = jnp.mean(scaled * unit, axis=-1, keepdims=True)
    back = inv * (scaled - jnp.mean(scaled, axis=-1, keepdims=True) - unit * inner)
    sums = jnp.concatenate([jnp.sum(grad * unit, axis=0, keepdims=True), jnp.sum(grad, axis=0, keepdims=True)], axis=0)
    return back, sums


def pick(flag, one, zero):
    return jnp.where(jnp.full(one.shape, flag, I32) == 1, one, zero)


class Far:
    def __init__(self, array):
        self.array = array


class Incoming:
    def __init__(self, source, here, sem):
        self.here, self.copy, self.waited = here, pltpu.make_async_copy(source, here, sem), False
        self.shape = here.shape
        self.copy.start()

    def finish(self):
        if not self.waited:
            self.copy.wait()
            self.waited = True

    def __getitem__(self, index):
        self.finish()
        return self.here[index]


class Outgoing:
    def __init__(self, target, here, sem):
        self.here, self.copy, self.sent = here, pltpu.make_async_copy(here, target, sem), False
        self.shape, self.dtype = here.shape, here.dtype

    def __setitem__(self, index, value):
        self.here[index] = value
        if index is Ellipsis:
            self.send()

    def __getitem__(self, index):
        return self.here[index]

    def send(self):
        if not self.sent:
            self.copy.start()
            self.sent = True


def call(kernel, outs, *args, scalars=(), after=(), scratch=(), **kw):
    far_in = [isinstance(a, Far) for a in args]
    far_out = [len(o) == 3 for o in outs]
    arrays = [a.array if f else a for a, f in zip(args, far_in)]
    buffers = [pltpu.VMEM(a.shape, a.dtype) for a, f in zip(arrays, far_in) if f]
    buffers += [pltpu.VMEM(o[0], o[1]) for o, f in zip(outs, far_out) if f]
    n_s, n_a, n_o, n_x, n_b = len(scalars), len(args), len(outs), len(scratch), len(buffers)

    def body(*refs):
        fixed, ins, refs = refs[:n_s], refs[n_s : n_s + n_a], refs[n_s + n_a + len(after) :]
        results, extra, refs = refs[:n_o], refs[n_o : n_o + n_x], refs[n_o + n_x :]
        copies = iter([(refs[i], refs[n_b].at[i]) for i in range(n_b)] if n_b else [])
        ins = [Incoming(r, *next(copies)) if f else r for r, f in zip(ins, far_in)]
        results = [Outgoing(r, *next(copies)) if f else r for r, f in zip(results, far_out)]
        kernel(*fixed, *ins, *results, *extra, **kw)
        for r, f in zip(ins, far_in):
            if f:
                r.finish()
        for r, f in zip(results, far_out):
            if f:
                r.send()
        for r, f in zip(results, far_out):
            if f:
                r.copy.wait()

    return pl.pallas_call(
        body,
        out_shape=[jax.ShapeDtypeStruct(o[0], o[1]) for o in outs],
        in_specs=[SMEM] * n_s + [HBM if f else VMEM for f in far_in] + [ANY] * len(after),
        out_specs=[HBM if f else VMEM for f in far_out],
        scratch_shapes=[pltpu.VMEM(x[0], x[1]) for x in scratch]
        + buffers
        + ([pltpu.SemaphoreType.DMA((n_b,))] if n_b else []),
        compiler_params=pltpu.CompilerParams(vmem_limit_bytes=32 * 1024 * 1024),
        cost_estimate=LIGHT if kernel in TAIL else LONG if kernel is ffn_final_kernel else COST,
        name=kernel.__name__,
    )(*scalars, *arrays, *after)


def far(shape):
    return (*shape, True)


ROWS_F = ((64, 768), F32)
ROWS_B = ((64, 768), BF)
PAIR_F = ((2, 768), F32)
BOTH_B = ((128, 768), BF)
CHUNKS = [ROWS_F, ROWS_B, ROWS_B, ROWS_B]
MORE_F = ((72, 768), F32)


def put_chunks(partial, refs):
    for j, ref in enumerate(refs):
        ref[...] = partial[64 * j : 64 * j + 64].astype(ref.dtype)


def add_chunks(refs):
    total = refs[0][...]
    for ref in refs[1:]:
        total = total + ref[...].astype(F32)
    return total


def all_rows(refs, part=None):
    cut = slice(None) if part is None else slice(64 * part, 64 * part + 64)
    return jnp.concatenate([ref[cut] for ref in refs], axis=0)


def entry_rows(at, tokens, norm):
    rows = tokens.astype(F32)
    return pick(at[0], rows, norm_forward(rows, norm[1, 0:1], norm[1, 1:2]))


def entry_kernel(at, arrived, norm, w_in, low, own_tokens, queries, kv):
    own_tokens[...] = arrived[at[4]]
    for j in range(4):
        low[64 * j : 64 * j + 64] = entry_rows(at, arrived[(at[4] + j) & 3], norm).astype(BF)
    low.send()
    packed = mm_nt(low[...], w_in[...])
    queries[...] = packed[:, :192].astype(BF)
    kv[...] = packed[:, 192:].astype(BF)


def cell_places(at, index, other_x, other_c):
    x, c, z = at[1] ^ other_x, at[3] ^ other_c, at[4]
    block = (x * 4 + ((index // 64 + z) & 3)) * 2 + c
    return block * 64 + (index & 63)


def documents(place, ends, slot):
    return sum((place >= ends[slot, d]).astype(I32) for d in range(3))


def score_bias(at, ends, query_slot, key_slot, causal):
    q_place = cell_places(at, lax.broadcasted_iota(I32, (1, 256), 1), 0, 0)
    q_doc = documents(q_place, ends, query_slot)
    out = []
    for chunk in range(4):
        k_place = cell_places(at, lax.broadcasted_iota(I32, (256, 1), 0), chunk // 2, chunk % 2)
        k_doc = documents(k_place, ends, key_slot)
        bias = jnp.where(k_doc == q_doc, 0.0, NEGATIVE)
        if causal:
            bias = jnp.where(k_place - q_place > (1 - at[0]) * 2048, NEGATIVE, bias)
        out.append(bias)
    return out


def attend_kernel(at, ends, queries, kv0, kv1, kv2, kv3, w_out, mixed, *chunks, cross):
    slot = (1, 0) if cross else (at[0], at[0])
    bias = score_bias(at, ends, slot[0], slot[1], not cross)
    kvs = (kv0, kv1, kv2, kv3)
    heads = []
    for h in range(3):
        cols = slice(64 * h, 64 * h + 64)
        vals = slice(192 + 64 * h, 256 + 64 * h)
        q = queries[:, cols]
        scores = [mm_nt(kv[:, cols], q) * 0.125 + b for kv, b in zip(kvs, bias)]
        top = functools.reduce(jnp.maximum, [jnp.max(s, axis=0, keepdims=True) for s in scores])
        weights = [jnp.exp(s - top) for s in scores]
        total = sum(jnp.sum(w, axis=0, keepdims=True) for w in weights)
        inv = 1.0 / total
        out = sum(mm_tn(kv[:, vals], (w * inv).astype(BF)) for kv, w in zip(kvs, weights))
        heads.append(out.T)
    joined = jnp.concatenate(heads, axis=1).astype(BF)
    mixed[...] = joined
    put_chunks(mm(joined, w_out[192:384] if cross else w_out[...]), chunks)


def attend_back_kernel(at, ends, g0, g1, g2, g3, queries, kv0, kv1, kv2, kv3, w_out, grad_q, keep, send, *, cross):
    slot = (1, 0) if cross else (at[0], at[0])
    bias = score_bias(at, ends, slot[0], slot[1], not cross)
    rows = all_rows((g0, g1, g2, g3), 0)
    grad_mixed = mm_nt(rows, w_out[192:384] if cross else w_out[...]).astype(BF)
    grads = []
    kvs = (kv0, kv1, kv2, kv3)
    for h in range(3):
        cols = slice(64 * h, 64 * h + 64)
        vals = slice(192 + 64 * h, 256 + 64 * h)
        q = queries[:, cols]
        g = grad_mixed[:, cols]
        scores = [mm_nt(kv[:, cols], q) * 0.125 + b for kv, b in zip(kvs, bias)]
        top = functools.reduce(jnp.maximum, [jnp.max(s, axis=0, keepdims=True) for s in scores])
        weights = [jnp.exp(s - top) for s in scores]
        inv = 1.0 / sum(jnp.sum(w, axis=0, keepdims=True) for w in weights)
        probs = [w * inv for w in weights]
        grad_probs = [mm_nt(kv[:, vals], g) for kv in kvs]
        inner = sum(jnp.sum(p * d, axis=0, keepdims=True) for p, d in zip(probs, grad_probs))
        raw = [(p * (d - inner) * 0.125).astype(BF) for p, d in zip(probs, grad_probs)]
        for chunk in range(4):
            ref = keep if chunk % 2 == 0 else send
            ref[chunk // 2, :, cols] = mm(raw[chunk], q).astype(ref.dtype)
            ref[chunk // 2, :, vals] = mm(probs[chunk].astype(BF), g).astype(ref.dtype)
        grads.append(sum(mm_tn(kv[:, cols], r) for kv, r in zip(kvs, raw)).T)
    grad_q[...] = jnp.concatenate(grads, axis=1).astype(BF)


def cut_kernel(left, right, up, down, sems):
    copies = [
        pltpu.make_async_copy(left.at[0:384], up, sems.at[0]),
        pltpu.make_async_copy(right.at[384:768], down, sems.at[1]),
    ]
    for copy in copies:
        copy.start()
    for copy in copies:
        copy.wait()


def first_norm_kernel(at, tokens, r0, r1, r2, r3, norm, sums, low):
    values = entry_rows(at, tokens[...], norm) + add_chunks((r0, r1, r2, r3))
    sums[...] = values
    low[...] = norm_forward(values, norm[0, 0:1], norm[0, 1:2]).astype(BF)


def cross_norm_kernel(base, r0, r1, r2, r3, norm, sums, after, low):
    values = norm_forward(base[...], norm[0, 0:1], norm[0, 1:2]) + add_chunks((r0, r1, r2, r3))
    sums[...] = values
    out = norm_forward(values, norm[1, 0:1], norm[1, 1:2])
    after[...] = out
    low[...] = out.astype(BF)


def memory_kernel(at, base, keep, got, norm, first, sums, low):
    values = norm_forward(base[...], norm[0, 0:1], norm[0, 1:2]) + keep[...] + got[...].astype(F32)
    sums[...] = values
    low[...] = pick(at[0], first[...].astype(F32), norm_forward(values, norm[2, 0:1], norm[2, 1:2])).astype(BF)


def pairs_kernel(a0, a1, a2, a3, w_cross, out):
    out[...] = mm_nt(all_rows((a0, a1, a2, a3)), w_cross[...]).astype(BF)


def query_kernel(a0, a1, a2, a3, w_cross, out):
    out[...] = mm_nt(all_rows((a0, a1, a2, a3)), w_cross[0:192]).astype(BF)


def shards(w0, w1, w3, up_2, down_2):
    for w in (w0, w1, w3):
        yield w[0:384], w[384:768]
    yield up_2[...], down_2[...]


def rows_up(rows, up):
    return mm(rows[:, :384], up[:, :384]) + mm(rows[:, 384:], up[:, 384:])


def ffn_kernel(own, other, w0, w1, w3, up_2, down_2, keep, send):
    rows = all_rows((own, other))
    total = 0.0
    for up, down in shards(w0, w1, w3, up_2, down_2):
        total = total + mm(gelu(rows_up(rows, up)).astype(BF), down)
    keep[...] = total[:64]
    send[...] = total[64:].astype(BF)


def ffn_back_kernel(own, other, g_own, g_other, w0, w1, w3, up_2, down_2, keep, send):
    rows = all_rows((own, other))
    grad = all_rows((g_own, g_other))
    left = right = 0.0
    for up, down in shards(w0, w1, w3, up_2, down_2):
        slope = gelu_slope(rows_up(rows, up))
        pre = (mm_nt(grad, down) * slope).astype(BF)
        left = left + mm_nt(pre, up[:, :384])
        right = right + mm_nt(pre, up[:, 384:])
    total = jnp.concatenate([left, right], axis=1)
    keep[...] = total[:64]
    send[...] = total[64:].astype(BF)


def turn_kernel(base, keep, got, cot, norm, decoded, grad, low):
    values = base[...] + keep[...] + got[...].astype(F32)
    unit, inv = normed(values)
    gain = norm[2, 0:1]
    decoded[...] = (unit * gain + norm[2, 1:2]).astype(BF)
    up = cot[...].astype(F32)
    scaled = up * gain
    inner = jnp.mean(scaled * unit, axis=-1, keepdims=True)
    back = inv * (scaled - jnp.mean(scaled, axis=-1, keepdims=True) - unit * inner)
    grad[0:64] = back
    grad[64:72] = below(jnp.concatenate([jnp.sum(up * unit, axis=0, keepdims=True), jnp.sum(up, axis=0, keepdims=True)], axis=0))
    low[...] = back.astype(BF)


def below(*pairs):
    blank = jnp.zeros((8 - 2 * len(pairs), 768), F32)
    return jnp.concatenate([*pairs, blank], axis=0)


def ffn_norm_back_kernel(base, keep, got, values, norm, grad, low):
    up = base[0:64] + keep[...] + got[...].astype(F32)
    back, sums = norm_backward(up, values[...], norm[1, 0:1])
    grad[0:64] = back
    grad[64:72] = below(sums, base[64:66])
    low[...] = back.astype(BF)


def add_core_kernel(keep, got, out_0, out_1):
    total = (keep[...] + got[...].astype(F32)).astype(BF)
    out_0[...] = total[0]
    out_1[...] = total[1]


def add_core_self_kernel(keep, got, own, send):
    total = keep[...] + got[...].astype(F32)
    own[...] = total[0]
    send[...] = total[1].astype(BF)


def project_back_kernel(at, m0, m1, grad_q, w_cross, grad_pairs, *chunks):
    total = (m0[...].astype(F32) + m1[...].astype(F32)).astype(BF)
    grad_pairs[...] = total
    mine = jnp.concatenate([grad_q[...], jnp.zeros((256, 192), BF)], axis=1)
    mine = pick(at[0], mine.astype(F32), total.astype(F32)).astype(BF)
    put_chunks(mm(mine, w_cross[...]), chunks)


def memory_back_kernel(at, r0, r1, r2, r3, values, norm, in_d, in_e, grad_d, total, grad, low, both):
    up = add_chunks((r0, r1, r2, r3))
    total[...] = up
    back, sums = norm_backward(up, values[...], norm[2, 0:1])
    grad[0:64] = back
    grad[64:72] = below(sums)
    low[...] = back.astype(BF)
    both[0:64] = pick(at[0], in_d[...].astype(F32), in_e[...].astype(F32)).astype(BF)
    both[64:128] = pick(at[0], grad_d[...].astype(F32), back).astype(BF)


def first_norm_back_kernel(at, grad_e, keep, got, grad_d, low_sum, values, norm, grad, low):
    enc = grad_e[0:64] + keep[...] + got[...].astype(F32)
    up = pick(at[0], grad_d[0:64] + low_sum[...], enc)
    back, sums = norm_backward(up, values[...], norm[0, 0:1])
    low[...] = back.astype(BF)
    grad[0:64] = back
    grad[64:72] = below(sums, grad_d[64:66], pick(at[0], grad_d[66:68], grad_e[64:66]))


def entry_back_kernel(grad_q, own, got, w_in, packed, *chunks):
    kv = (own[...] + got[...].astype(F32)).astype(BF)
    packed[...] = jnp.concatenate([grad_q[...], kv], axis=1)
    put_chunks(mm(packed[...], w_in[...]), chunks)


def last_norm_back_kernel(at, r0, r1, r2, r3, base, tokens, norm, decoded, memory_sums, out):
    up = base[0:64] + add_chunks((r0, r1, r2, r3))
    back, sums = norm_backward(up, tokens[...].astype(F32), norm[1, 0:1])
    out[0:64] = pick(at[0], up, back).astype(BF)
    memory = norm_forward(memory_sums[...], norm[2, 0:1], norm[2, 1:2])
    out[64:128] = pick(at[0], decoded[...].astype(F32), memory).astype(BF)
    pairs = below(base[64:66], pick(at[0], base[66:68], sums), base[68:70])
    out[128:144] = two_parts(pairs)


def two_parts(values):
    high = values.astype(BF).astype(F32)
    return jnp.concatenate([high, values - high], axis=0).astype(BF)


def one_part(rows):
    rows = rows.astype(F32)
    return rows[:8] + rows[8:]


def collect_kernel(at, p0, p1, p2, p3, sums):
    parts = jnp.zeros((4, 8, 768), F32)
    place = lax.broadcasted_iota(I32, (4, 8, 768), 0)
    for j, ref in enumerate((p0, p1, p2, p3)):
        parts = jnp.where(place == ((at[4] + j) & 3), one_part(ref[128:144])[None], parts)
    sums[...] = (parts[0] + parts[1]) + (parts[2] + parts[3])


def pack_kernel(at, p0, p1, p2, p3, sums, xh_sums, own, got, chunks):
    norms = two_parts(sums[...] + xh_sums[...])
    total = (own[...].astype(F32) + got[...].astype(F32)).astype(BF)
    for j, ref in enumerate((p0, p1, p2, p3)):
        chunks[(at[4] + j) & 3, 0:128] = ref[0:128]
        chunks[j, 128:144] = norms
        chunks[j, 144:240] = total


def unpack_kernel(chunks, grads, outs, norms, half):
    for micro in range(4):
        grads[micro] = chunks[micro, 0:64].astype(F32)
        outs[micro] = chunks[micro, 64:128]
        half[96 * micro : 96 * micro + 96] = chunks[micro, 144:240]
    parts = [one_part(chunks[y, 128:144]) for y in range(4)]
    norms[...] = (parts[0] + parts[1]) + (parts[2] + parts[3])


def split_core(full, at, keep, send):
    half = keep.shape[0]
    keep[...] = full[pl.ds(pl.multiple_of(at[3] * half, 16), half)]
    send[...] = full[pl.ds(pl.multiple_of((1 - at[3]) * half, 16), half)]


def ffn_weights_kernel(at, *refs):
    late, passed, crossed = (refs[4 * i : 4 * i + 4] for i in range(3))
    grad_pairs, grad_q, mixed, w_up, w_down, keep, send, full = refs[12:]
    flag = at[0]

    def choose(one, zero):
        return pick(flag, one.astype(F32), zero.astype(F32)).astype(BF)

    rows = all_rows(late, 0)
    grad = all_rows(late, 1)
    first = all_rows(passed)
    full[1536:1728] = mm_tn(choose(grad_q[...], grad_pairs[:, :192]), first).astype(BF)
    full[1728:1920] = mm_tn(choose(mixed[...], grad_pairs[:, 192:]), choose(all_rows(crossed), first)).astype(BF)
    pre = mm(rows, w_up[...])
    full[768:1536] = mm_tn(gelu(pre).astype(BF), grad).astype(BF)
    grad_pre = (mm_nt(grad, w_down[...]) * gelu_slope(pre)).astype(BF)
    full[0:768] = mm_tn(rows, grad_pre).astype(BF)
    split_core(full, at, keep, send)


def attn_weights_kernel(at, low, packed, mixed, g0, g1, g2, g3, keep, send, full):
    full[576:768] = mm_tn(mixed[...], all_rows((g0, g1, g2, g3), 0)).astype(BF)
    full[0:576] = mm_tn(packed[...], low[...]).astype(BF)
    split_core(full, at, keep, send)


def add_two_kernel(keep, got, out):
    rows = out.shape[1]
    for y in range(4):
        cut = slice(rows * y, rows * y + rows)
        out[y] = (keep[cut].astype(F32) + got[cut].astype(F32)).astype(BF)


def add_four_kernel(parts, out):
    total = (parts[0].astype(F32) + parts[1].astype(F32)) + (parts[2].astype(F32) + parts[3].astype(F32))
    out[...] = total.astype(out.dtype)


def add_all_kernel(*refs):
    total = refs[0][...].astype(F32)
    for ref in refs[1:-1]:
        total = total + ref[...].astype(F32)
    refs[-1][...] = total.astype(refs[-1].dtype)


def join_y_kernel(at, t0, t1, t2, t3, half):
    rows = t0.shape[0]
    for j, ref in enumerate((t0, t1, t2, t3)):
        half[pl.ds(pl.multiple_of(((at[2] + j) & 3) * rows, 16), rows)] = ref[...]


def join_core(at, own, got, full):
    half = own.shape[0]
    full[pl.ds(pl.multiple_of(at[3] * half, 16), half)] = own[...]
    full[pl.ds(pl.multiple_of((1 - at[3]) * half, 16), half)] = got[...]


def ffn_final_kernel(at, own, got, up, down, cross, full):
    join_core(at, own, got, full)
    up[...] = full[0:768].astype(F32)
    down[...] = full[768:1536].astype(F32)
    cross[...] = full[1536:1920].astype(F32)


def attn_final_kernel(at, own, got, grad_in, grad_out, full):
    join_core(at, own, got, full)
    grad_in[...] = full[0:576].astype(F32)
    grad_out[...] = full[576:768].astype(F32)


def reduce_y(keep, got, after=()):
    rows, cols = keep.shape
    (total,) = call(add_two_kernel, [((4, rows // 4, cols), BF)], keep, got, after=after)
    return total, lax.all_to_all(total, "y", 0, 0)


def add_four(parts, after=()):
    return call(add_four_kernel, [(parts.shape[1:], BF)], parts, after=after)[0]


def add_parts(parts, after=()):
    return call(add_all_kernel, [(parts[0].shape, BF)], *parts, after=after)[0]


TAIL = (
    last_norm_back_kernel,
    collect_kernel,
    pack_kernel,
    add_two_kernel,
    add_four_kernel,
    add_all_kernel,
    join_y_kernel,
    unpack_kernel,
)


def add_sums(one, two):
    return call(add_all_kernel, [((8, 768), F32)], one, two)[0]


def gather_y(at, total, after=()):
    parts = [total] + [shift(total, "y", -j) for j in range(1, 4)]
    rows, cols = total.shape
    return call(join_y_kernel, [((rows * 4, cols), BF)], *parts, scalars=(at,), after=after)[0]


def halves(at, w_up, w_down):
    def body(at, w_up, w_down, both, sems):
        first = pl.multiple_of(at[3] * 384, 128)
        copies = [
            pltpu.make_async_copy(w_up.at[0:384, pl.ds(first, 384)], both.at[0:384, 0:384], sems.at[0]),
            pltpu.make_async_copy(w_up.at[384:768, pl.ds(first, 384)], both.at[0:384, 384:768], sems.at[1]),
            pltpu.make_async_copy(w_down.at[pl.ds(first, 384)], both.at[384:768], sems.at[2]),
        ]
        for copy in copies:
            copy.start()
        for copy in copies:
            copy.wait()

    return pl.pallas_call(
        body,
        out_shape=jax.ShapeDtypeStruct((768, 768), BF),
        in_specs=[SMEM, HBM, HBM],
        out_specs=VMEM,
        scratch_shapes=[pltpu.SemaphoreType.DMA((3,))],
        cost_estimate=COST,
        name="halves_kernel",
    )(at, w_up, w_down)


def cut(left, right, after):
    def body(left, right, *refs):
        cut_kernel(left, right, *refs[len(after) :])

    return pl.pallas_call(
        body,
        out_shape=[jax.ShapeDtypeStruct((384, 768), BF)] * 2,
        in_specs=[HBM] * 2 + [ANY] * len(after),
        out_specs=[VMEM] * 2,
        scratch_shapes=[pltpu.SemaphoreType.DMA((2,))],
        cost_estimate=COST,
        name="cut_kernel",
    )(left, right, *after)


def per_device(tokens, segments, cotangent, attn_in, attn_out, ffn_in, ffn_out, cross_proj, norms):
    w_in = Far(jnp.transpose(attn_in[0], (1, 2, 0)).reshape(576, 768))
    w_out = Far(attn_out[0])
    w_up = ffn_in[0]
    w_down = ffn_out[0]
    w_cross = Far(jnp.transpose(cross_proj[0], (1, 2, 0)).reshape(384, 768))
    norm = Far(norms[0])
    sec = lax.axis_index("section")
    x_at = lax.axis_index("xh")
    y_at = lax.axis_index("y")
    c_at = lax.axis_index("core")
    z_at = lax.axis_index("tensor")
    dec = sec == 1
    at = jnp.stack([sec, x_at, y_at, c_at, z_at]).astype(I32)
    here = (at,)

    arrived = lax.all_to_all(tokens[0, :, 0], "y", 0, 0)
    seg_micro = lax.dynamic_index_in_dim(segments[:, :, 0], y_at, 1, keepdims=False)
    ends = jnp.sum((seg_micro[:, None, :] <= jnp.arange(3, dtype=I32)[None, :, None]).astype(I32), axis=2)
    places = (at, ends)

    w_0 = halves(at, w_up, w_down)
    w_3, w_1 = shift(w_0, "tensor", 1), shift(w_0, "tensor", -1)

    entry_low, tok_own, queries, kv = call(
        entry_kernel,
        [far(((256, 768), BF)), far(ROWS_B), ((256, 192), BF), ((256, 384), BF)],
        arrived,
        norm,
        w_in,
        scalars=here,
        after=(w_0, ends),
    )
    cot_pairs = [(a * 4 + b, b * 4 + a) for a in range(4) for b in range(4)]
    cot_send = lax.dynamic_index_in_dim(cotangent[:, 0], z_at, 0, keepdims=False)
    cot_own = lax.ppermute(cot_send, ("y", "tensor"), cot_pairs)
    kv_x = shift(kv, "xh", 1)
    self_kv = (kv, swap_core(kv), kv_x, swap_core(kv_x))
    mixed, *chunks = call(
        attend_kernel, [far(((256, 192), BF))] + CHUNKS, queries, *self_kv, w_out, scalars=places, after=(cot_own,), cross=False
    )
    up_send, down_send = cut(w_3, w_1, (kv_x,))
    weights = [Far(w) for w in (w_0, w_1, w_3, shift(up_send, "tensor", 1), shift(down_send, "tensor", -1))]
    sums0, after_self_low = call(
        first_norm_kernel, [far(ROWS_F), ROWS_B], Far(tok_own), *scatter_z(chunks), norm, scalars=here
    )

    after_self_other = swap_core(after_self_low)
    keep, send = call(ffn_kernel, [ROWS_F, ROWS_B], after_self_low, after_self_other, *weights)
    sums2, passed = call(
        memory_kernel, [far(ROWS_F), ROWS_B], Far(sums0), keep, swap_core(send), norm, after_self_low, scalars=here
    )
    passed_all = gather_z(passed)
    (pairs,) = call(pairs_kernel, [((256, 384), BF)], *passed_all, w_cross)
    m0 = lax.ppermute(pairs, ("section", "xh"), section_pairs(0, 1, 0))
    m1 = lax.ppermute(pairs, ("section", "xh"), section_pairs(0, 1, 1))
    memory_kv = (m0, swap_core(m0), m1, swap_core(m1))
    (cross_q,) = call(query_kernel, [((256, 192), BF)], *passed_all, w_cross, after=(pairs,))

    mixed_cross, *chunks = call(
        attend_kernel, [far(((256, 192), BF))] + CHUNKS, cross_q, *memory_kv, w_cross, scalars=places, cross=True
    )
    sums1, after_cross, after_cross_low = call(
        cross_norm_kernel, [ROWS_F, ROWS_F, ROWS_B], Far(sums0), *scatter_z(chunks), norm
    )
    after_cross_other = swap_core(after_cross_low)
    keep, send = call(ffn_kernel, [ROWS_F, ROWS_B], after_cross_low, after_cross_other, *weights)
    decoded, grad_d2, grad_ffn_d = call(
        turn_kernel, [far(ROWS_B), MORE_F, ROWS_B], after_cross, keep, swap_core(send), Far(cot_own), norm
    )

    keep, send = call(
        ffn_back_kernel,
        [ROWS_F, ROWS_B],
        after_cross_low,
        after_cross_other,
        grad_ffn_d,
        swap_core(grad_ffn_d),
        *weights,
    )
    grad_d1, grad_d1_low = call(
        ffn_norm_back_kernel, [far(MORE_F), ROWS_B], grad_d2, keep, swap_core(send), sums1, norm
    )
    grad_crossed_all = gather_z(grad_d1_low)
    pair_f, pair_b = ((2, 256, 384), F32), ((2, 256, 384), BF)
    grad_q_cross, keep, send = call(
        attend_back_kernel,
        [((256, 192), BF), pair_f, pair_b],
        *grad_crossed_all,
        cross_q,
        *memory_kv,
        w_cross,
        scalars=places,
        cross=True,
    )
    to_0, to_1 = call(add_core_kernel, [((256, 384), BF)] * 2, keep, swap_core(send))
    g0 = lax.ppermute(to_0, ("section", "xh"), section_pairs(1, 0, 0))
    g1 = lax.ppermute(to_1, ("section", "xh"), section_pairs(1, 0, 1))

    grad_pairs, *chunks = call(
        project_back_kernel, [((256, 384), BF)] + CHUNKS, g0, g1, grad_q_cross, w_cross, scalars=here
    )
    low_sum, grad_e2, grad_ffn_e, both = call(
        memory_back_kernel,
        [ROWS_F, MORE_F, ROWS_B, BOTH_B],
        *scatter_z(chunks),
        Far(sums2),
        norm,
        after_cross_low,
        after_self_low,
        grad_ffn_d,
        scalars=here,
    )
    both_all = gather_z(both)
    keep, send = call(
        ffn_back_kernel,
        [ROWS_F, ROWS_B],
        after_self_low,
        after_self_other,
        grad_ffn_e,
        swap_core(grad_ffn_e),
        *weights,
    )
    grad_0, grad_0_low = call(
        first_norm_back_kernel,
        [far(MORE_F), ROWS_B],
        grad_e2,
        keep,
        swap_core(send),
        Far(grad_d1),
        low_sum,
        Far(sums0),
        norm,
        scalars=here,
    )
    grad_sa_all = gather_z(grad_0_low)

    half = ((960, 768), BF)
    w_keep, w_send = call(
        ffn_weights_kernel,
        [half, half],
        *both_all,
        *passed_all,
        *grad_crossed_all,
        grad_pairs,
        grad_q_cross,
        Far(mixed_cross),
        Far(w_up),
        Far(w_down),
        scalars=here,
        scratch=[((1920, 768), BF)],
        after=grad_sa_all,
    )

    grad_q, keep, send = call(
        attend_back_kernel,
        [((256, 192), BF), pair_f, pair_b],
        *grad_sa_all,
        queries,
        *self_kv,
        w_out,
        scalars=places,
        after=(w_keep,),
        cross=False,
    )
    w_sent, w_parts = reduce_y(w_keep, swap_core(w_send), after=(grad_q,))
    own_kv, send_kv = call(
        add_core_self_kernel, [((256, 384), F32), ((256, 384), BF)], keep, swap_core(send)
    )
    grad_packed, *chunks = call(
        entry_back_kernel,
        [((256, 576), BF)] + CHUNKS,
        grad_q,
        own_kv,
        shift(send_kv, "xh", 1),
        w_in,
        after=(w_sent,),
    )
    got_chunks = scatter_z(chunks)
    half = ((384, 768), BF)
    a_keep, a_send = call(
        attn_weights_kernel,
        [half, half],
        Far(entry_low),
        grad_packed,
        Far(mixed),
        *grad_sa_all,
        scalars=here,
        scratch=[((768, 768), BF)],
    )
    (grad_own,) = call(
        last_norm_back_kernel,
        [((144, 768), BF)],
        *got_chunks,
        Far(grad_0),
        Far(tok_own),
        norm,
        Far(decoded),
        Far(sums2),
        scalars=here,
        after=(a_keep,),
    )
    own_all = gather_z(grad_own)
    a_sent, a_parts = reduce_y(a_keep, swap_core(a_send), after=(grad_own,))
    w_piece = add_four(w_parts, after=(grad_own,))
    w_total = add_parts([w_piece, shift(w_piece, "xh", 1)], after=own_all[1:])
    a_piece = add_four(a_parts, after=(w_piece,))
    a_got = shift(a_piece, "xh", 1)
    (sums,) = call(collect_kernel, [((8, 768), F32)], *own_all, scalars=here, after=(w_total,))
    sums = add_sums(sums, swap_core(sums))
    xh_sums = shift(sums, "xh", 1)
    (packed_out,) = call(
        pack_kernel,
        [((4, 240, 768), BF)],
        *own_all,
        sums,
        xh_sums,
        a_piece,
        a_got,
        scalars=here,
    )
    unpacked = lax.all_to_all(packed_out, "y", 0, 0)
    w_half = gather_y(at, w_total, after=(a_got, xh_sums))
    grad_up, grad_down, grad_cross = call(
        ffn_final_kernel,
        [far(((768, 768), F32)), far(((768, 768), F32)), far(((384, 768), F32))],
        w_half,
        swap_core(w_half),
        scalars=here,
        scratch=[((1920, 768), BF)],
    )
    token_grads, outputs, norm_sums, a_half = call(
        unpack_kernel,
        [far(((4, 64, 768), F32)), far(((4, 64, 768), BF)), far(((8, 768), F32)), ((384, 768), BF)],
        unpacked,
        after=(grad_up,),
    )
    grad_in, grad_out = call(
        attn_final_kernel,
        [far(((576, 768), F32)), far(((192, 768), F32))],
        a_half,
        swap_core(a_half),
        scalars=here,
        scratch=[((768, 768), BF)],
    )
    return (
        outputs[None, :, None],
        token_grads[None, :, None],
        jnp.transpose(grad_in.reshape(3, 192, 768), (2, 0, 1))[None],
        grad_out[None],
        grad_up[None],
        grad_down[None],
        jnp.transpose(grad_cross.reshape(2, 192, 768), (2, 0, 1))[None],
        norm_sums[:6].reshape(1, 3, 2, 768),
    )


def solution(mesh):
    fine = Mesh(mesh.devices.reshape(2, 2, 4, 2, 4), ("section", "xh", "y", "core", "tensor"))
    dp = ("xh", "y", "core")
    weights = (
        P("section", None, None, "tensor"),
        P("section", "tensor", None),
        P("section", None, "tensor"),
        P("section", "tensor", None),
        P("section", None, None, "tensor"),
        P("section", None, None, None),
    )
    rows = P("section", None, None, dp, None)
    return jax.shard_map(
        per_device,
        mesh=fine,
        in_specs=(rows, P(), P(None, None, dp, None)) + weights,
        out_specs=(rows, rows) + weights,
        check_vma=False,
    )
```

```python
import functools
import math

import jax
import jax.numpy as jnp
from jax import lax
from jax.experimental import pallas as pl
from jax.experimental.pallas import tpu as pltpu
from jax.sharding import Mesh, PartitionSpec as P

EPSILON = 1e-05
NEGATIVE = -1e30
BF = jnp.bfloat16
F32 = jnp.float32
I32 = jnp.int32
ROOT_HALF = 1.0 / math.sqrt(2.0)
DENSITY = 1.0 / math.sqrt(2.0 * math.pi)
VMEM = pl.BlockSpec(memory_space=pltpu.VMEM)
SMEM = pl.BlockSpec(memory_space=pltpu.SMEM)
ANY = pl.BlockSpec(memory_space=pl.ANY)
HBM = pl.BlockSpec(memory_space=pltpu.HBM)
COST = pl.CostEstimate(flops=2_000_000_000, bytes_accessed=0, transcendentals=0)
LONG = pl.CostEstimate(flops=8_000_000_000, bytes_accessed=0, transcendentals=0)
LIGHT = pl.CostEstimate(flops=1000, bytes_accessed=0, transcendentals=0)


def shift(value, axis, steps):
    count = lax.axis_size(axis)
    return lax.ppermute(value, axis, [(i, (i + steps) % count) for i in range(count)])


def swap_core(value):
    return shift(value, "core", 1)


def section_pairs(own, other, flip):
    return [(own * 2 + i, other * 2 + (i ^ flip)) for i in range(2)]


def gather_z(rows):
    return [rows] + [shift(rows, "tensor", -j) for j in range(1, 4)]


def scatter_z(chunks):
    return [chunks[0]] + [shift(chunks[j], "tensor", j) for j in range(1, 4)]


def mm(a, b):
    return jnp.dot(a, b, preferred_element_type=F32)


def mm_nt(a, b):
    return lax.dot_general(a, b, (((1,), (1,)), ((), ())), preferred_element_type=F32)


def mm_tn(a, b):
    return lax.dot_general(a, b, (((0,), (0,)), ((), ())), preferred_element_type=F32)


def erf(v):
    v = jnp.clip(v, -4.0, 4.0)
    w = v * v
    top = -2.72614225801306e-10
    for c in (2.77068142495902e-08, -2.10102402082508e-06, -5.69250639462346e-05, -7.34990630326855e-04,
              -2.95459980854025e-03, -1.60960333262415e-02):
        top = top * w + c
    low = -1.45660718464996e-05
    for c in (-2.13374055278905e-04, -1.68282697438203e-03, -7.37332916720468e-03, -1.42647390514189e-02):
        low = low * w + c
    return v * top / low


def gelu(v):
    return v * (0.5 + 0.5 * erf(v * ROOT_HALF))


def gelu_slope(v):
    return 0.5 + 0.5 * erf(v * ROOT_HALF) + v * (jnp.exp(-0.5 * v * v) * DENSITY)


def normed(values):
    centered = values - jnp.mean(values, axis=-1, keepdims=True)
    inv = lax.rsqrt(jnp.mean(centered * centered, axis=-1, keepdims=True) + EPSILON)
    return centered * inv, inv


def norm_forward(values, gain, bias):
    return normed(values)[0] * gain + bias


def norm_backward(grad, values, gain):
    unit, inv = normed(values)
    scaled = grad * gain
    inner = jnp.mean(scaled * unit, axis=-1, keepdims=True)
    back = inv * (scaled - jnp.mean(scaled, axis=-1, keepdims=True) - unit * inner)
    sums = jnp.concatenate([jnp.sum(grad * unit, axis=0, keepdims=True), jnp.sum(grad, axis=0, keepdims=True)], axis=0)
    return back, sums


def pick(flag, one, zero):
    return jnp.where(jnp.full(one.shape, flag, I32) == 1, one, zero)


class Far:
    def __init__(self, array):
        self.array = array


class Incoming:
    def __init__(self, source, here, sem):
        self.here, self.copy, self.waited = here, pltpu.make_async_copy(source, here, sem), False
        self.shape = here.shape
        self.copy.start()

    def finish(self):
        if not self.waited:
            self.copy.wait()
            self.waited = True

    def __getitem__(self, index):
        self.finish()
        return self.here[index]


class Outgoing:
    def __init__(self, target, here, sem):
        self.here, self.copy, self.sent = here, pltpu.make_async_copy(here, target, sem), False
        self.shape, self.dtype = here.shape, here.dtype

    def __setitem__(self, index, value):
        self.here[index] = value
        if index is Ellipsis:
            self.send()

    def __getitem__(self, index):
        return self.here[index]

    def send(self):
        if not self.sent:
            self.copy.start()
            self.sent = True


def call(kernel, outs, *args, scalars=(), after=(), scratch=(), **kw):
    far_in = [isinstance(a, Far) for a in args]
    far_out = [len(o) == 3 for o in outs]
    arrays = [a.array if f else a for a, f in zip(args, far_in)]
    buffers = [pltpu.VMEM(a.shape, a.dtype) for a, f in zip(arrays, far_in) if f]
    buffers += [pltpu.VMEM(o[0], o[1]) for o, f in zip(outs, far_out) if f]
    n_s, n_a, n_o, n_x, n_b = len(scalars), len(args), len(outs), len(scratch), len(buffers)

    def body(*refs):
        fixed, ins, refs = refs[:n_s], refs[n_s : n_s + n_a], refs[n_s + n_a + len(after) :]
        results, extra, refs = refs[:n_o], refs[n_o : n_o + n_x], refs[n_o + n_x :]
        copies = iter([(refs[i], refs[n_b].at[i]) for i in range(n_b)] if n_b else [])
        ins = [Incoming(r, *next(copies)) if f else r for r, f in zip(ins, far_in)]
        results = [Outgoing(r, *next(copies)) if f else r for r, f in zip(results, far_out)]
        kernel(*fixed, *ins, *results, *extra, **kw)
        for r, f in zip(ins, far_in):
            if f:
                r.finish()
        for r, f in zip(results, far_out):
            if f:
                r.send()
        for r, f in zip(results, far_out):
            if f:
                r.copy.wait()

    return pl.pallas_call(
        body,
        out_shape=[jax.ShapeDtypeStruct(o[0], o[1]) for o in outs],
        in_specs=[SMEM] * n_s + [HBM if f else VMEM for f in far_in] + [ANY] * len(after),
        out_specs=[HBM if f else VMEM for f in far_out],
        scratch_shapes=[pltpu.VMEM(x[0], x[1]) for x in scratch]
        + buffers
        + ([pltpu.SemaphoreType.DMA((n_b,))] if n_b else []),
        compiler_params=pltpu.CompilerParams(vmem_limit_bytes=32 * 1024 * 1024),
        cost_estimate=KIND.get(kernel, LIGHT if kernel in TAIL else COST),
        name=kernel.__name__,
    )(*scalars, *arrays, *after)


def far(shape):
    return (*shape, True)


ROWS_F = ((64, 768), F32)
ROWS_B = ((64, 768), BF)
PAIR_F = ((2, 768), F32)
BOTH_B = ((128, 768), BF)
CHUNKS = [ROWS_F, ROWS_B, ROWS_B, ROWS_B]
MORE_F = ((72, 768), F32)


def put_chunks(partial, refs):
    for j, ref in enumerate(refs):
        ref[...] = partial[64 * j : 64 * j + 64].astype(ref.dtype)


def add_chunks(refs):
    total = refs[0][...]
    for ref in refs[1:]:
        total = total + ref[...].astype(F32)
    return total


def all_rows(refs, part=None):
    cut = slice(None) if part is None else slice(64 * part, 64 * part + 64)
    return jnp.concatenate([ref[cut] for ref in refs], axis=0)


def entry_rows(at, tokens, norm):
    rows = tokens.astype(F32)
    return pick(at[0], rows, norm_forward(rows, norm[1, 0:1], norm[1, 1:2]))


def entry_kernel(at, arrived, norm, w_in, low, own_tokens, queries, kv):
    own_tokens[...] = arrived[at[4]]
    for j in range(4):
        low[64 * j : 64 * j + 64] = entry_rows(at, arrived[(at[4] + j) & 3], norm).astype(BF)
    low.send()
    packed = mm_nt(low[...], w_in[...])
    queries[...] = packed[:, :192].astype(BF)
    kv[...] = packed[:, 192:].astype(BF)


def cell_places(at, index, other_x, other_c):
    x, c, z = at[1] ^ other_x, at[3] ^ other_c, at[4]
    block = (x * 4 + ((index // 64 + z) & 3)) * 2 + c
    return block * 64 + (index & 63)


def documents(place, ends, slot):
    return sum((place >= ends[slot, d]).astype(I32) for d in range(3))


def score_bias(at, ends, query_slot, key_slot, causal):
    q_place = cell_places(at, lax.broadcasted_iota(I32, (1, 256), 1), 0, 0)
    q_doc = documents(q_place, ends, query_slot)
    out = []
    for chunk in range(4):
        k_place = cell_places(at, lax.broadcasted_iota(I32, (256, 1), 0), chunk // 2, chunk % 2)
        k_doc = documents(k_place, ends, key_slot)
        bias = jnp.where(k_doc == q_doc, 0.0, NEGATIVE)
        if causal:
            bias = jnp.where(k_place - q_place > (1 - at[0]) * 2048, NEGATIVE, bias)
        out.append(bias)
    return out


def attend_kernel(at, ends, queries, kv0, kv1, kv2, kv3, w_out, mixed, *chunks, cross):
    slot = (1, 0) if cross else (at[0], at[0])
    bias = score_bias(at, ends, slot[0], slot[1], not cross)
    kvs = (kv0, kv1, kv2, kv3)
    heads = []
    for h in range(3):
        cols = slice(64 * h, 64 * h + 64)
        vals = slice(192 + 64 * h, 256 + 64 * h)
        q = queries[:, cols]
        scores = [mm_nt(kv[:, cols], q) * 0.125 + b for kv, b in zip(kvs, bias)]
        top = functools.reduce(jnp.maximum, [jnp.max(s, axis=0, keepdims=True) for s in scores])
        weights = [jnp.exp(s - top) for s in scores]
        total = sum(jnp.sum(w, axis=0, keepdims=True) for w in weights)
        inv = 1.0 / total
        out = sum(mm_tn(kv[:, vals], (w * inv).astype(BF)) for kv, w in zip(kvs, weights))
        heads.append(out.T)
    joined = jnp.concatenate(heads, axis=1).astype(BF)
    mixed[...] = joined
    put_chunks(mm(joined, w_out[192:384] if cross else w_out[...]), chunks)


def attend_back_kernel(at, ends, g0, g1, g2, g3, queries, kv0, kv1, kv2, kv3, w_out, grad_q, keep, send, *, cross):
    slot = (1, 0) if cross else (at[0], at[0])
    bias = score_bias(at, ends, slot[0], slot[1], not cross)
    rows = all_rows((g0, g1, g2, g3), 0)
    grad_mixed = mm_nt(rows, w_out[192:384] if cross else w_out[...]).astype(BF)
    grads = []
    kvs = (kv0, kv1, kv2, kv3)
    for h in range(3):
        cols = slice(64 * h, 64 * h + 64)
        vals = slice(192 + 64 * h, 256 + 64 * h)
        q = queries[:, cols]
        g = grad_mixed[:, cols]
        scores = [mm_nt(kv[:, cols], q) * 0.125 + b for kv, b in zip(kvs, bias)]
        top = functools.reduce(jnp.maximum, [jnp.max(s, axis=0, keepdims=True) for s in scores])
        weights = [jnp.exp(s - top) for s in scores]
        inv = 1.0 / sum(jnp.sum(w, axis=0, keepdims=True) for w in weights)
        probs = [w * inv for w in weights]
        grad_probs = [mm_nt(kv[:, vals], g) for kv in kvs]
        inner = sum(jnp.sum(p * d, axis=0, keepdims=True) for p, d in zip(probs, grad_probs))
        raw = [(p * (d - inner) * 0.125).astype(BF) for p, d in zip(probs, grad_probs)]
        for chunk in range(4):
            ref = keep if chunk % 2 == 0 else send
            ref[chunk // 2, :, cols] = mm(raw[chunk], q).astype(ref.dtype)
            ref[chunk // 2, :, vals] = mm(probs[chunk].astype(BF), g).astype(ref.dtype)
        grads.append(sum(mm_tn(kv[:, cols], r) for kv, r in zip(kvs, raw)).T)
    grad_q[...] = jnp.concatenate(grads, axis=1).astype(BF)


def cut_kernel(left, right, up, down, sems):
    copies = [
        pltpu.make_async_copy(left.at[0:384], up, sems.at[0]),
        pltpu.make_async_copy(right.at[384:768], down, sems.at[1]),
    ]
    for copy in copies:
        copy.start()
    for copy in copies:
        copy.wait()


def first_norm_kernel(at, tokens, r0, r1, r2, r3, norm, sums, low):
    values = entry_rows(at, tokens[...], norm) + add_chunks((r0, r1, r2, r3))
    sums[...] = values
    low[...] = norm_forward(values, norm[0, 0:1], norm[0, 1:2]).astype(BF)


def cross_norm_kernel(base, r0, r1, r2, r3, norm, sums, after, low):
    values = norm_forward(base[...], norm[0, 0:1], norm[0, 1:2]) + add_chunks((r0, r1, r2, r3))
    sums[...] = values
    out = norm_forward(values, norm[1, 0:1], norm[1, 1:2])
    after[...] = out
    low[...] = out.astype(BF)


def memory_kernel(at, base, keep, got, norm, first, sums, low):
    values = norm_forward(base[...], norm[0, 0:1], norm[0, 1:2]) + keep[...] + got[...].astype(F32)
    sums[...] = values
    low[...] = pick(at[0], first[...].astype(F32), norm_forward(values, norm[2, 0:1], norm[2, 1:2])).astype(BF)


def pairs_kernel(a0, a1, a2, a3, w_cross, out):
    out[...] = mm_nt(all_rows((a0, a1, a2, a3)), w_cross[...]).astype(BF)


def query_kernel(a0, a1, a2, a3, w_cross, out):
    out[...] = mm_nt(all_rows((a0, a1, a2, a3)), w_cross[0:192]).astype(BF)


def shards(w0, w1, w3, up_2, down_2):
    for w in (w0, w1, w3):
        yield w[0:384], w[384:768]
    yield up_2[...], down_2[...]


def rows_up(rows, up):
    return mm(rows[:, :384], up[:, :384]) + mm(rows[:, 384:], up[:, 384:])


def ffn_kernel(own, other, w0, w1, w3, up_2, down_2, keep, send):
    rows = all_rows((own, other))
    total = 0.0
    for up, down in shards(w0, w1, w3, up_2, down_2):
        total = total + mm(gelu(rows_up(rows, up)).astype(BF), down)
    keep[...] = total[:64]
    send[...] = total[64:].astype(BF)


def ffn_back_kernel(own, other, g_own, g_other, w0, w1, w3, up_2, down_2, keep, send):
    rows = all_rows((own, other))
    grad = all_rows((g_own, g_other))
    left = right = 0.0
    for up, down in shards(w0, w1, w3, up_2, down_2):
        slope = gelu_slope(rows_up(rows, up))
        pre = (mm_nt(grad, down) * slope).astype(BF)
        left = left + mm_nt(pre, up[:, :384])
        right = right + mm_nt(pre, up[:, 384:])
    total = jnp.concatenate([left, right], axis=1)
    keep[...] = total[:64]
    send[...] = total[64:].astype(BF)


def turn_kernel(base, keep, got, cot, norm, decoded, grad, low):
    values = base[...] + keep[...] + got[...].astype(F32)
    unit, inv = normed(values)
    gain = norm[2, 0:1]
    decoded[...] = (unit * gain + norm[2, 1:2]).astype(BF)
    up = cot[...].astype(F32)
    scaled = up * gain
    inner = jnp.mean(scaled * unit, axis=-1, keepdims=True)
    back = inv * (scaled - jnp.mean(scaled, axis=-1, keepdims=True) - unit * inner)
    grad[0:64] = back
    grad[64:72] = below(jnp.concatenate([jnp.sum(up * unit, axis=0, keepdims=True), jnp.sum(up, axis=0, keepdims=True)], axis=0))
    low[...] = back.astype(BF)


def below(*pairs):
    blank = jnp.zeros((8 - 2 * len(pairs), 768), F32)
    return jnp.concatenate([*pairs, blank], axis=0)


def ffn_norm_back_kernel(base, keep, got, values, norm, grad, low):
    up = base[0:64] + keep[...] + got[...].astype(F32)
    back, sums = norm_backward(up, values[...], norm[1, 0:1])
    grad[0:64] = back
    grad[64:72] = below(sums, base[64:66])
    low[...] = back.astype(BF)


def add_core_kernel(keep, got, out_0, out_1):
    total = (keep[...].astype(F32) + got[...].astype(F32)).astype(BF)
    out_0[...] = total[0]
    out_1[...] = total[1]


def add_core_self_kernel(keep, got, own, send):
    total = keep[...].astype(F32) + got[...].astype(F32)
    own[...] = total[0]
    send[...] = total[1].astype(BF)


def project_back_kernel(at, m0, m1, grad_q, w_cross, grad_pairs, *chunks):
    total = (m0[...].astype(F32) + m1[...].astype(F32)).astype(BF)
    grad_pairs[...] = total
    mine = jnp.concatenate([grad_q[...], jnp.zeros((256, 192), BF)], axis=1)
    mine = pick(at[0], mine.astype(F32), total.astype(F32)).astype(BF)
    put_chunks(mm(mine, w_cross[...]), chunks)


def memory_back_kernel(at, r0, r1, r2, r3, values, norm, in_d, in_e, grad_d, total, grad, low, both):
    up = add_chunks((r0, r1, r2, r3))
    total[...] = up
    back, sums = norm_backward(up, values[...], norm[2, 0:1])
    grad[0:64] = back
    grad[64:72] = below(sums)
    low[...] = back.astype(BF)
    both[0:64] = pick(at[0], in_d[...].astype(F32), in_e[...].astype(F32)).astype(BF)
    both[64:128] = pick(at[0], grad_d[...].astype(F32), back).astype(BF)


def first_norm_back_kernel(at, grad_e, keep, got, grad_d, low_sum, values, norm, grad, low):
    enc = grad_e[0:64] + keep[...] + got[...].astype(F32)
    up = pick(at[0], grad_d[0:64] + low_sum[...], enc)
    back, sums = norm_backward(up, values[...], norm[0, 0:1])
    low[...] = back.astype(BF)
    grad[0:64] = back
    grad[64:72] = below(sums, grad_d[64:66], pick(at[0], grad_d[66:68], grad_e[64:66]))


def entry_back_kernel(grad_q, own, got, w_in, packed, *chunks):
    kv = (own[...] + got[...].astype(F32)).astype(BF)
    packed[...] = jnp.concatenate([grad_q[...], kv], axis=1)
    put_chunks(mm(packed[...], w_in[...]), chunks)


def last_norm_back_kernel(at, r0, r1, r2, r3, base, tokens, norm, decoded, memory_sums, out):
    up = base[0:64] + add_chunks((r0, r1, r2, r3))
    back, sums = norm_backward(up, tokens[...].astype(F32), norm[1, 0:1])
    out[0:64] = pick(at[0], up, back).astype(BF)
    memory = norm_forward(memory_sums[...], norm[2, 0:1], norm[2, 1:2])
    out[64:128] = pick(at[0], decoded[...].astype(F32), memory).astype(BF)
    pairs = below(base[64:66], pick(at[0], base[66:68], sums), base[68:70])
    out[128:144] = two_parts(pairs)


def two_parts(values):
    high = values.astype(BF).astype(F32)
    return jnp.concatenate([high, values - high], axis=0).astype(BF)


def one_part(rows):
    rows = rows.astype(F32)
    return rows[:8] + rows[8:]


def collect_kernel(at, p0, p1, p2, p3, sums):
    parts = jnp.zeros((4, 8, 768), F32)
    place = lax.broadcasted_iota(I32, (4, 8, 768), 0)
    for j, ref in enumerate((p0, p1, p2, p3)):
        parts = jnp.where(place == ((at[4] + j) & 3), one_part(ref[128:144])[None], parts)
    sums[...] = (parts[0] + parts[1]) + (parts[2] + parts[3])


def rows_pack_kernel(at, p0, p1, p2, p3, chunks):
    for j, ref in enumerate((p0, p1, p2, p3)):
        chunks[(at[4] + j) & 3] = ref[0:128]


def rows_out_kernel(chunks, grads, outs):
    for micro in range(4):
        grads[micro] = chunks[micro, 0:64].astype(F32)
        outs[micro] = chunks[micro, 64:128]


def pack_kernel(sums, xh_sums, own, got, chunks):
    norms = two_parts(sums[...] + xh_sums[...])
    total = (own[...].astype(F32) + got[...].astype(F32)).astype(BF)
    for y in range(4):
        chunks[y, 0:16] = norms
        chunks[y, 16:112] = total


def unpack_kernel(chunks, norms, half):
    for y in range(4):
        half[96 * y : 96 * y + 96] = chunks[y, 16:112]
    parts = [one_part(chunks[y, 0:16]) for y in range(4)]
    norms[...] = (parts[0] + parts[1]) + (parts[2] + parts[3])


def split_core(full, at, keep, send):
    half = keep.shape[0]
    keep[...] = full[pl.ds(pl.multiple_of(at[3] * half, 16), half)]
    send[...] = full[pl.ds(pl.multiple_of((1 - at[3]) * half, 16), half)]


def ffn_weights_kernel(at, *refs):
    late, passed, crossed = (refs[4 * i : 4 * i + 4] for i in range(3))
    grad_pairs, grad_q, mixed, w_up, w_down, keep, send, full = refs[12:]
    flag = at[0]

    def choose(one, zero):
        return pick(flag, one.astype(F32), zero.astype(F32)).astype(BF)

    rows = all_rows(late, 0)
    grad = all_rows(late, 1)
    first = all_rows(passed)
    full[1536:1728] = mm_tn(choose(grad_q[...], grad_pairs[:, :192]), first).astype(BF)
    full[1728:1920] = mm_tn(choose(mixed[...], grad_pairs[:, 192:]), choose(all_rows(crossed), first)).astype(BF)
    pre = mm(rows, w_up[...])
    full[768:1536] = mm_tn(gelu(pre).astype(BF), grad).astype(BF)
    grad_pre = (mm_nt(grad, w_down[...]) * gelu_slope(pre)).astype(BF)
    full[0:768] = mm_tn(rows, grad_pre).astype(BF)
    split_core(full, at, keep, send)


def attn_weights_kernel(at, low, packed, mixed, g0, g1, g2, g3, keep, send, full):
    full[576:768] = mm_tn(mixed[...], all_rows((g0, g1, g2, g3), 0)).astype(BF)
    full[0:576] = mm_tn(packed[...], low[...]).astype(BF)
    split_core(full, at, keep, send)


def add_two_kernel(keep, got, out):
    rows = out.shape[1]
    for y in range(4):
        cut = slice(rows * y, rows * y + rows)
        out[y] = (keep[cut].astype(F32) + got[cut].astype(F32)).astype(BF)


def add_four_kernel(parts, out):
    total = (parts[0].astype(F32) + parts[1].astype(F32)) + (parts[2].astype(F32) + parts[3].astype(F32))
    out[...] = total.astype(out.dtype)


def add_all_kernel(*refs):
    total = refs[0][...].astype(F32)
    for ref in refs[1:-1]:
        total = total + ref[...].astype(F32)
    refs[-1][...] = total.astype(refs[-1].dtype)


def join_y_kernel(at, t0, t1, t2, t3, half):
    rows = t0.shape[0]
    for j, ref in enumerate((t0, t1, t2, t3)):
        half[pl.ds(pl.multiple_of(((at[2] + j) & 3) * rows, 16), rows)] = ref[...]


def join_core(at, own, got, full):
    half = own.shape[0]
    full[pl.ds(pl.multiple_of(at[3] * half, 16), half)] = own[...]
    full[pl.ds(pl.multiple_of((1 - at[3]) * half, 16), half)] = got[...]


def ffn_final_kernel(at, own, got, up, down, cross, full):
    join_core(at, own, got, full)
    up[...] = full[0:768].astype(F32)
    down[...] = full[768:1536].astype(F32)
    cross[...] = full[1536:1920].astype(F32)


def attn_final_kernel(at, own, got, grad_in, grad_out, full):
    join_core(at, own, got, full)
    grad_in[...] = full[0:576].astype(F32)
    grad_out[...] = full[576:768].astype(F32)


def reduce_y(keep, got, after=()):
    rows, cols = keep.shape
    (total,) = call(add_two_kernel, [((4, rows // 4, cols), BF)], keep, got, after=after)
    return total, lax.all_to_all(total, "y", 0, 0)


def add_four(parts, after=()):
    return call(add_four_kernel, [(parts.shape[1:], BF)], parts, after=after)[0]


def add_parts(parts, after=()):
    return call(add_all_kernel, [(parts[0].shape, BF)], *parts, after=after)[0]


KIND = {ffn_final_kernel: LONG, attn_weights_kernel: COST, entry_back_kernel: COST}
TAIL = (
    last_norm_back_kernel,
    collect_kernel,
    pack_kernel,
    rows_pack_kernel,
    rows_out_kernel,
    add_two_kernel,
    add_four_kernel,
    add_all_kernel,
    join_y_kernel,
    unpack_kernel,
)


def add_sums(one, two):
    return call(add_all_kernel, [((8, 768), F32)], one, two)[0]


def gather_y(at, total, after=()):
    parts = [total] + [shift(total, "y", -j) for j in range(1, 4)]
    rows, cols = total.shape
    return call(join_y_kernel, [((rows * 4, cols), BF)], *parts, scalars=(at,), after=after)[0]


def halves(at, w_up, w_down):
    def body(at, w_up, w_down, both, sems):
        first = pl.multiple_of(at[3] * 384, 128)
        copies = [
            pltpu.make_async_copy(w_up.at[0:384, pl.ds(first, 384)], both.at[0:384, 0:384], sems.at[0]),
            pltpu.make_async_copy(w_up.at[384:768, pl.ds(first, 384)], both.at[0:384, 384:768], sems.at[1]),
            pltpu.make_async_copy(w_down.at[pl.ds(first, 384)], both.at[384:768], sems.at[2]),
        ]
        for copy in copies:
            copy.start()
        for copy in copies:
            copy.wait()

    return pl.pallas_call(
        body,
        out_shape=jax.ShapeDtypeStruct((768, 768), BF),
        in_specs=[SMEM, HBM, HBM],
        out_specs=VMEM,
        scratch_shapes=[pltpu.SemaphoreType.DMA((3,))],
        cost_estimate=COST,
        name="halves_kernel",
    )(at, w_up, w_down)


def cut(left, right, after):
    def body(left, right, *refs):
        cut_kernel(left, right, *refs[len(after) :])

    return pl.pallas_call(
        body,
        out_shape=[jax.ShapeDtypeStruct((384, 768), BF)] * 2,
        in_specs=[HBM] * 2 + [ANY] * len(after),
        out_specs=[VMEM] * 2,
        scratch_shapes=[pltpu.SemaphoreType.DMA((2,))],
        cost_estimate=COST,
        name="cut_kernel",
    )(left, right, *after)


def per_device(tokens, segments, cotangent, attn_in, attn_out, ffn_in, ffn_out, cross_proj, norms):
    w_in = Far(jnp.transpose(attn_in[0], (1, 2, 0)).reshape(576, 768))
    w_out = Far(attn_out[0])
    w_up = ffn_in[0]
    w_down = ffn_out[0]
    w_cross = Far(jnp.transpose(cross_proj[0], (1, 2, 0)).reshape(384, 768))
    norm = Far(norms[0])
    sec = lax.axis_index("section")
    x_at = lax.axis_index("xh")
    y_at = lax.axis_index("y")
    c_at = lax.axis_index("core")
    z_at = lax.axis_index("tensor")
    dec = sec == 1
    at = jnp.stack([sec, x_at, y_at, c_at, z_at]).astype(I32)
    here = (at,)

    arrived = lax.all_to_all(tokens[0, :, 0], "y", 0, 0)
    seg_micro = lax.dynamic_index_in_dim(segments[:, :, 0], y_at, 1, keepdims=False)
    ends = jnp.sum((seg_micro[:, None, :] <= jnp.arange(3, dtype=I32)[None, :, None]).astype(I32), axis=2)
    places = (at, ends)

    w_0 = halves(at, w_up, w_down)
    w_3, w_1 = shift(w_0, "tensor", 1), shift(w_0, "tensor", -1)

    entry_low, tok_own, queries, kv = call(
        entry_kernel,
        [far(((256, 768), BF)), far(ROWS_B), ((256, 192), BF), ((256, 384), BF)],
        arrived,
        norm,
        w_in,
        scalars=here,
    )
    cot_pairs = [(a * 4 + b, b * 4 + a) for a in range(4) for b in range(4)]
    cot_send = lax.dynamic_index_in_dim(cotangent[:, 0], z_at, 0, keepdims=False)
    cot_own = lax.ppermute(cot_send, ("y", "tensor"), cot_pairs)
    kv_x = shift(kv, "xh", 1)
    self_kv = (kv, swap_core(kv), kv_x, swap_core(kv_x))
    mixed, *chunks = call(
        attend_kernel, [far(((256, 192), BF))] + CHUNKS, queries, *self_kv, w_out, scalars=places, after=(cot_own,), cross=False
    )
    up_send, down_send = cut(w_3, w_1, (kv,))
    weights = [Far(w) for w in (w_0, w_1, w_3, shift(up_send, "tensor", 1), shift(down_send, "tensor", -1))]
    sums0, after_self_low = call(
        first_norm_kernel, [far(ROWS_F), ROWS_B], Far(tok_own), *scatter_z(chunks), norm, scalars=here
    )

    after_self_other = swap_core(after_self_low)
    keep, send = call(ffn_kernel, [ROWS_F, ROWS_B], after_self_low, after_self_other, *weights)
    sums2, passed = call(
        memory_kernel, [far(ROWS_F), ROWS_B], Far(sums0), keep, swap_core(send), norm, after_self_low, scalars=here
    )
    passed_all = gather_z(passed)
    (pairs,) = call(pairs_kernel, [((256, 384), BF)], *passed_all, w_cross)
    m0 = lax.ppermute(pairs, ("section", "xh"), section_pairs(0, 1, 0))
    m1 = lax.ppermute(pairs, ("section", "xh"), section_pairs(0, 1, 1))
    memory_kv = (m0, swap_core(m0), m1, swap_core(m1))
    (cross_q,) = call(query_kernel, [((256, 192), BF)], *passed_all, w_cross, after=(pairs,))

    mixed_cross, *chunks = call(
        attend_kernel, [far(((256, 192), BF))] + CHUNKS, cross_q, *memory_kv, w_cross, scalars=places, cross=True
    )
    sums1, after_cross, after_cross_low = call(
        cross_norm_kernel, [ROWS_F, ROWS_F, ROWS_B], Far(sums0), *scatter_z(chunks), norm
    )
    after_cross_other = swap_core(after_cross_low)
    keep, send = call(ffn_kernel, [ROWS_F, ROWS_B], after_cross_low, after_cross_other, *weights)
    decoded, grad_d2, grad_ffn_d = call(
        turn_kernel, [far(ROWS_B), MORE_F, ROWS_B], after_cross, keep, swap_core(send), Far(cot_own), norm
    )

    keep, send = call(
        ffn_back_kernel,
        [ROWS_F, ROWS_B],
        after_cross_low,
        after_cross_other,
        grad_ffn_d,
        swap_core(grad_ffn_d),
        *weights,
    )
    grad_d1, grad_d1_low = call(
        ffn_norm_back_kernel, [far(MORE_F), ROWS_B], grad_d2, keep, swap_core(send), sums1, norm
    )
    grad_crossed_all = gather_z(grad_d1_low)
    pair_b = ((2, 256, 384), BF)
    grad_q_cross, keep, send = call(
        attend_back_kernel,
        [((256, 192), BF), pair_b, pair_b],
        *grad_crossed_all,
        cross_q,
        *memory_kv,
        w_cross,
        scalars=places,
        cross=True,
    )
    to_0, to_1 = call(add_core_kernel, [((256, 384), BF)] * 2, keep, swap_core(send))
    g0 = lax.ppermute(to_0, ("section", "xh"), section_pairs(1, 0, 0))
    g1 = lax.ppermute(to_1, ("section", "xh"), section_pairs(1, 0, 1))

    grad_pairs, *chunks = call(
        project_back_kernel, [((256, 384), BF)] + CHUNKS, g0, g1, grad_q_cross, w_cross, scalars=here
    )
    low_sum, grad_e2, grad_ffn_e, both = call(
        memory_back_kernel,
        [ROWS_F, MORE_F, ROWS_B, BOTH_B],
        *scatter_z(chunks),
        Far(sums2),
        norm,
        after_cross_low,
        after_self_low,
        grad_ffn_d,
        scalars=here,
    )
    both_all = gather_z(both)
    keep, send = call(
        ffn_back_kernel,
        [ROWS_F, ROWS_B],
        after_self_low,
        after_self_other,
        grad_ffn_e,
        swap_core(grad_ffn_e),
        *weights,
    )
    grad_0, grad_0_low = call(
        first_norm_back_kernel,
        [far(MORE_F), ROWS_B],
        grad_e2,
        keep,
        swap_core(send),
        Far(grad_d1),
        low_sum,
        Far(sums0),
        norm,
        scalars=here,
    )
    grad_sa_all = gather_z(grad_0_low)

    half = ((960, 768), BF)
    w_keep, w_send = call(
        ffn_weights_kernel,
        [half, half],
        *both_all,
        *passed_all,
        *grad_crossed_all,
        grad_pairs,
        grad_q_cross,
        Far(mixed_cross),
        Far(w_up),
        Far(w_down),
        scalars=here,
        scratch=[((1920, 768), BF)],
        after=grad_sa_all,
    )

    grad_q, keep, send = call(
        attend_back_kernel,
        [((256, 192), BF), pair_b, pair_b],
        *grad_sa_all,
        queries,
        *self_kv,
        w_out,
        scalars=places,
        after=(w_keep,),
        cross=False,
    )
    own_kv, send_kv = call(
        add_core_self_kernel, [((256, 384), F32), ((256, 384), BF)], keep, swap_core(send)
    )
    w_sent, w_parts = reduce_y(w_keep, swap_core(w_send), after=(own_kv, grad_q))
    grad_packed, *chunks = call(
        entry_back_kernel,
        [((256, 576), BF)] + CHUNKS,
        grad_q,
        own_kv,
        shift(send_kv, "xh", 1),
        w_in,
        after=(w_sent,),
    )
    got_chunks = scatter_z(chunks)
    half = ((384, 768), BF)
    a_keep, a_send = call(
        attn_weights_kernel,
        [half, half],
        Far(entry_low),
        grad_packed,
        Far(mixed),
        *grad_sa_all,
        scalars=here,
        scratch=[((768, 768), BF)],
    )
    (grad_own,) = call(
        last_norm_back_kernel,
        [((144, 768), BF)],
        *got_chunks,
        Far(grad_0),
        Far(tok_own),
        norm,
        Far(decoded),
        Far(sums2),
        scalars=here,
        after=(a_keep,),
    )
    own_all = gather_z(grad_own)
    a_sent, a_parts = reduce_y(a_keep, swap_core(a_send), after=(grad_own,))
    w_piece = add_four(w_parts, after=(grad_own,))
    w_total = add_parts([w_piece, shift(w_piece, "xh", 1)], after=own_all[1:])
    a_piece = add_four(a_parts, after=(grad_own,))
    a_got = shift(a_piece, "xh", 1)
    (row_chunks,) = call(rows_pack_kernel, [((4, 128, 768), BF)], *own_all, scalars=here)
    token_grads, outputs = call(
        rows_out_kernel,
        [far(((4, 64, 768), F32)), far(((4, 64, 768), BF))],
        lax.all_to_all(row_chunks, "y", 0, 0),
    )
    (sums,) = call(collect_kernel, [((8, 768), F32)], *own_all, scalars=here, after=(w_total,))
    sums = add_sums(sums, swap_core(sums))
    xh_sums = shift(sums, "xh", 1)
    (packed_out,) = call(
        pack_kernel,
        [((4, 112, 768), BF)],
        sums,
        xh_sums,
        a_piece,
        a_got,
    )
    unpacked = lax.all_to_all(packed_out, "y", 0, 0)
    w_half = gather_y(at, w_total, after=(packed_out, token_grads))
    grad_up, grad_down, grad_cross = call(
        ffn_final_kernel,
        [far(((768, 768), F32)), far(((768, 768), F32)), far(((384, 768), F32))],
        w_half,
        swap_core(w_half),
        scalars=here,
        scratch=[((1920, 768), BF)],
    )
    norm_sums, a_half = call(
        unpack_kernel,
        [far(((8, 768), F32)), ((384, 768), BF)],
        unpacked,
        after=(grad_up,),
    )
    grad_in, grad_out = call(
        attn_final_kernel,
        [far(((576, 768), F32)), far(((192, 768), F32))],
        a_half,
        swap_core(a_half),
        scalars=here,
        scratch=[((768, 768), BF)],
    )
    return (
        outputs[None, :, None],
        token_grads[None, :, None],
        jnp.transpose(grad_in.reshape(3, 192, 768), (2, 0, 1))[None],
        grad_out[None],
        grad_up[None],
        grad_down[None],
        jnp.transpose(grad_cross.reshape(2, 192, 768), (2, 0, 1))[None],
        norm_sums[:6].reshape(1, 3, 2, 768),
    )


def solution(mesh):
    fine = Mesh(mesh.devices.reshape(2, 2, 4, 2, 4), ("section", "xh", "y", "core", "tensor"))
    dp = ("xh", "y", "core")
    weights = (
        P("section", None, None, "tensor"),
        P("section", "tensor", None),
        P("section", None, "tensor"),
        P("section", "tensor", None),
        P("section", None, None, "tensor"),
        P("section", None, None, None),
    )
    rows = P("section", None, None, dp, None)
    return jax.shard_map(
        per_device,
        mesh=fine,
        in_specs=(rows, P(), P(None, None, dp, None)) + weights,
        out_specs=(rows, rows) + weights,
        check_vma=False,
    )
```

```python
import functools
import math

import jax
import jax.numpy as jnp
from jax import lax
from jax.experimental import pallas as pl
from jax.experimental.pallas import tpu as pltpu
from jax.sharding import Mesh, PartitionSpec as P

EPSILON = 1e-05
NEGATIVE = -1e30
BF = jnp.bfloat16
F32 = jnp.float32
I32 = jnp.int32
ROOT_HALF = 1.0 / math.sqrt(2.0)
DENSITY = 1.0 / math.sqrt(2.0 * math.pi)
VMEM = pl.BlockSpec(memory_space=pltpu.VMEM)
SMEM = pl.BlockSpec(memory_space=pltpu.SMEM)
ANY = pl.BlockSpec(memory_space=pl.ANY)
HBM = pl.BlockSpec(memory_space=pltpu.HBM)
COST = pl.CostEstimate(flops=2_000_000_000, bytes_accessed=0, transcendentals=0)
LONG = pl.CostEstimate(flops=8_000_000_000, bytes_accessed=0, transcendentals=0)
LIGHT = pl.CostEstimate(flops=1000, bytes_accessed=0, transcendentals=0)


def shift(value, axis, steps):
    count = lax.axis_size(axis)
    return lax.ppermute(value, axis, [(i, (i + steps) % count) for i in range(count)])


def swap_core(value):
    return shift(value, "core", 1)


def section_pairs(own, other, flip):
    return [(own * 2 + i, other * 2 + (i ^ flip)) for i in range(2)]


def gather_z(rows):
    return [rows] + [shift(rows, "tensor", -j) for j in range(1, 4)]


def scatter_z(chunks):
    return [chunks[0]] + [shift(chunks[j], "tensor", j) for j in range(1, 4)]


def mm(a, b):
    return jnp.dot(a, b, preferred_element_type=F32)


def mm_nt(a, b):
    return lax.dot_general(a, b, (((1,), (1,)), ((), ())), preferred_element_type=F32)


def mm_tn(a, b):
    return lax.dot_general(a, b, (((0,), (0,)), ((), ())), preferred_element_type=F32)


def erf(v):
    v = jnp.clip(v, -4.0, 4.0)
    w = v * v
    top = -2.72614225801306e-10
    for c in (2.77068142495902e-08, -2.10102402082508e-06, -5.69250639462346e-05, -7.34990630326855e-04,
              -2.95459980854025e-03, -1.60960333262415e-02):
        top = top * w + c
    low = -1.45660718464996e-05
    for c in (-2.13374055278905e-04, -1.68282697438203e-03, -7.37332916720468e-03, -1.42647390514189e-02):
        low = low * w + c
    return v * top / low


def gelu(v):
    return v * (0.5 + 0.5 * erf(v * ROOT_HALF))


def gelu_slope(v):
    return 0.5 + 0.5 * erf(v * ROOT_HALF) + v * (jnp.exp(-0.5 * v * v) * DENSITY)


def normed(values):
    centered = values - jnp.mean(values, axis=-1, keepdims=True)
    inv = lax.rsqrt(jnp.mean(centered * centered, axis=-1, keepdims=True) + EPSILON)
    return centered * inv, inv


def norm_forward(values, gain, bias):
    return normed(values)[0] * gain + bias


def norm_backward(grad, values, gain):
    unit, inv = normed(values)
    scaled = grad * gain
    inner = jnp.mean(scaled * unit, axis=-1, keepdims=True)
    back = inv * (scaled - jnp.mean(scaled, axis=-1, keepdims=True) - unit * inner)
    sums = jnp.concatenate([jnp.sum(grad * unit, axis=0, keepdims=True), jnp.sum(grad, axis=0, keepdims=True)], axis=0)
    return back, sums


def pick(flag, one, zero):
    return jnp.where(jnp.full(one.shape, flag, I32) == 1, one, zero)


class Far:
    def __init__(self, array):
        self.array = array


class Incoming:
    def __init__(self, source, here, sem):
        self.here, self.copy, self.waited = here, pltpu.make_async_copy(source, here, sem), False
        self.shape = here.shape
        self.copy.start()

    def finish(self):
        if not self.waited:
            self.copy.wait()
            self.waited = True

    def __getitem__(self, index):
        self.finish()
        return self.here[index]


class Outgoing:
    def __init__(self, target, here, sem):
        self.here, self.copy, self.sent = here, pltpu.make_async_copy(here, target, sem), False
        self.shape, self.dtype = here.shape, here.dtype

    def __setitem__(self, index, value):
        self.here[index] = value
        if index is Ellipsis:
            self.send()

    def __getitem__(self, index):
        return self.here[index]

    def send(self):
        if not self.sent:
            self.copy.start()
            self.sent = True


def call(kernel, outs, *args, scalars=(), after=(), scratch=(), **kw):
    far_in = [isinstance(a, Far) for a in args]
    far_out = [len(o) == 3 for o in outs]
    arrays = [a.array if f else a for a, f in zip(args, far_in)]
    buffers = [pltpu.VMEM(a.shape, a.dtype) for a, f in zip(arrays, far_in) if f]
    buffers += [pltpu.VMEM(o[0], o[1]) for o, f in zip(outs, far_out) if f]
    n_s, n_a, n_o, n_x, n_b = len(scalars), len(args), len(outs), len(scratch), len(buffers)

    def body(*refs):
        fixed, ins, refs = refs[:n_s], refs[n_s : n_s + n_a], refs[n_s + n_a + len(after) :]
        results, extra, refs = refs[:n_o], refs[n_o : n_o + n_x], refs[n_o + n_x :]
        copies = iter([(refs[i], refs[n_b].at[i]) for i in range(n_b)] if n_b else [])
        ins = [Incoming(r, *next(copies)) if f else r for r, f in zip(ins, far_in)]
        results = [Outgoing(r, *next(copies)) if f else r for r, f in zip(results, far_out)]
        kernel(*fixed, *ins, *results, *extra, **kw)
        for r, f in zip(ins, far_in):
            if f:
                r.finish()
        for r, f in zip(results, far_out):
            if f:
                r.send()
        for r, f in zip(results, far_out):
            if f:
                r.copy.wait()

    return pl.pallas_call(
        body,
        out_shape=[jax.ShapeDtypeStruct(o[0], o[1]) for o in outs],
        in_specs=[SMEM] * n_s + [HBM if f else VMEM for f in far_in] + [ANY] * len(after),
        out_specs=[HBM if f else VMEM for f in far_out],
        scratch_shapes=[pltpu.VMEM(x[0], x[1]) for x in scratch]
        + buffers
        + ([pltpu.SemaphoreType.DMA((n_b,))] if n_b else []),
        compiler_params=pltpu.CompilerParams(vmem_limit_bytes=32 * 1024 * 1024),
        cost_estimate=KIND.get(kernel, LIGHT if kernel in TAIL else COST),
        name=kernel.__name__,
    )(*scalars, *arrays, *after)


def far(shape):
    return (*shape, True)


ROWS_F = ((64, 768), F32)
ROWS_B = ((64, 768), BF)
PAIR_F = ((2, 768), F32)
BOTH_B = ((128, 768), BF)
CHUNKS = [ROWS_F, ROWS_B, ROWS_B, ROWS_B]
MORE_F = ((72, 768), F32)


def put_chunks(partial, refs):
    for j, ref in enumerate(refs):
        ref[...] = partial[64 * j : 64 * j + 64].astype(ref.dtype)


def add_chunks(refs):
    total = refs[0][...]
    for ref in refs[1:]:
        total = total + ref[...].astype(F32)
    return total


def all_rows(refs, part=None):
    cut = slice(None) if part is None else slice(64 * part, 64 * part + 64)
    return jnp.concatenate([ref[cut] for ref in refs], axis=0)


def entry_rows(at, tokens, norm):
    rows = tokens.astype(F32)
    return pick(at[0], rows, norm_forward(rows, norm[1, 0:1], norm[1, 1:2]))


def entry_kernel(at, arrived, norm, w_in, low, own_tokens, queries, kv):
    own_tokens[...] = arrived[at[4]]
    for j in range(4):
        low[64 * j : 64 * j + 64] = entry_rows(at, arrived[(at[4] + j) & 3], norm).astype(BF)
    low.send()
    packed = mm_nt(low[...], w_in[...])
    queries[...] = packed[:, :192].astype(BF)
    kv[...] = packed[:, 192:].astype(BF)


def cell_places(at, index, other_x, other_c):
    x, c, z = at[1] ^ other_x, at[3] ^ other_c, at[4]
    block = (x * 4 + ((index // 64 + z) & 3)) * 2 + c
    return block * 64 + (index & 63)


def documents(place, ends, slot):
    return sum((place >= ends[slot, d]).astype(I32) for d in range(3))


def score_bias(at, ends, query_slot, key_slot, causal):
    q_place = cell_places(at, lax.broadcasted_iota(I32, (1, 256), 1), 0, 0)
    q_doc = documents(q_place, ends, query_slot)
    out = []
    for chunk in range(4):
        k_place = cell_places(at, lax.broadcasted_iota(I32, (256, 1), 0), chunk // 2, chunk % 2)
        k_doc = documents(k_place, ends, key_slot)
        bias = jnp.where(k_doc == q_doc, 0.0, NEGATIVE)
        if causal:
            bias = jnp.where(k_place - q_place > (1 - at[0]) * 2048, NEGATIVE, bias)
        out.append(bias)
    return out


def attend_kernel(at, ends, queries, kv0, kv1, kv2, kv3, w_out, mixed, *chunks, cross):
    slot = (1, 0) if cross else (at[0], at[0])
    bias = score_bias(at, ends, slot[0], slot[1], not cross)
    kvs = (kv0, kv1, kv2, kv3)
    heads = []
    for h in range(3):
        cols = slice(64 * h, 64 * h + 64)
        vals = slice(192 + 64 * h, 256 + 64 * h)
        q = queries[:, cols]
        scores = [mm_nt(kv[:, cols], q) * 0.125 + b for kv, b in zip(kvs, bias)]
        top = functools.reduce(jnp.maximum, [jnp.max(s, axis=0, keepdims=True) for s in scores])
        weights = [jnp.exp(s - top) for s in scores]
        total = sum(jnp.sum(w, axis=0, keepdims=True) for w in weights)
        inv = 1.0 / total
        out = sum(mm_tn(kv[:, vals], (w * inv).astype(BF)) for kv, w in zip(kvs, weights))
        heads.append(out.T)
    joined = jnp.concatenate(heads, axis=1).astype(BF)
    mixed[...] = joined
    put_chunks(mm(joined, w_out[192:384] if cross else w_out[...]), chunks)


def attend_back_kernel(at, ends, g0, g1, g2, g3, queries, kv0, kv1, kv2, kv3, w_out, grad_q, keep, send, *, cross):
    slot = (1, 0) if cross else (at[0], at[0])
    bias = score_bias(at, ends, slot[0], slot[1], not cross)
    rows = all_rows((g0, g1, g2, g3), 0)
    grad_mixed = mm_nt(rows, w_out[192:384] if cross else w_out[...]).astype(BF)
    grads = []
    kvs = (kv0, kv1, kv2, kv3)
    for h in range(3):
        cols = slice(64 * h, 64 * h + 64)
        vals = slice(192 + 64 * h, 256 + 64 * h)
        q = queries[:, cols]
        g = grad_mixed[:, cols]
        scores = [mm_nt(kv[:, cols], q) * 0.125 + b for kv, b in zip(kvs, bias)]
        top = functools.reduce(jnp.maximum, [jnp.max(s, axis=0, keepdims=True) for s in scores])
        weights = [jnp.exp(s - top) for s in scores]
        inv = 1.0 / sum(jnp.sum(w, axis=0, keepdims=True) for w in weights)
        probs = [w * inv for w in weights]
        grad_probs = [mm_nt(kv[:, vals], g) for kv in kvs]
        inner = sum(jnp.sum(p * d, axis=0, keepdims=True) for p, d in zip(probs, grad_probs))
        raw = [(p * (d - inner) * 0.125).astype(BF) for p, d in zip(probs, grad_probs)]
        for chunk in range(4):
            ref = keep if chunk % 2 == 0 else send
            ref[chunk // 2, :, cols] = mm(raw[chunk], q).astype(ref.dtype)
            ref[chunk // 2, :, vals] = mm(probs[chunk].astype(BF), g).astype(ref.dtype)
        grads.append(sum(mm_tn(kv[:, cols], r) for kv, r in zip(kvs, raw)).T)
    grad_q[...] = jnp.concatenate(grads, axis=1).astype(BF)


def cut_kernel(left, right, up, down, sems):
    copies = [
        pltpu.make_async_copy(left.at[0:384], up, sems.at[0]),
        pltpu.make_async_copy(right.at[384:768], down, sems.at[1]),
    ]
    for copy in copies:
        copy.start()
    for copy in copies:
        copy.wait()


def first_norm_kernel(at, tokens, r0, r1, r2, r3, norm, sums, low):
    values = entry_rows(at, tokens[...], norm) + add_chunks((r0, r1, r2, r3))
    sums[...] = values
    low[...] = norm_forward(values, norm[0, 0:1], norm[0, 1:2]).astype(BF)


def cross_norm_kernel(base, r0, r1, r2, r3, norm, sums, after, low):
    values = norm_forward(base[...], norm[0, 0:1], norm[0, 1:2]) + add_chunks((r0, r1, r2, r3))
    sums[...] = values
    out = norm_forward(values, norm[1, 0:1], norm[1, 1:2])
    after[...] = out
    low[...] = out.astype(BF)


def memory_kernel(at, base, keep, got, norm, first, sums, low):
    values = norm_forward(base[...], norm[0, 0:1], norm[0, 1:2]) + keep[...] + got[...].astype(F32)
    sums[...] = values
    low[...] = pick(at[0], first[...].astype(F32), norm_forward(values, norm[2, 0:1], norm[2, 1:2])).astype(BF)


def pairs_kernel(a0, a1, a2, a3, w_cross, out):
    out[...] = mm_nt(all_rows((a0, a1, a2, a3)), w_cross[...]).astype(BF)


def query_kernel(a0, a1, a2, a3, w_cross, out):
    out[...] = mm_nt(all_rows((a0, a1, a2, a3)), w_cross[0:192]).astype(BF)


def shards(w0, w1, w3, up_2, down_2):
    for w in (w0, w1, w3):
        yield w[0:384], w[384:768]
    yield up_2[...], down_2[...]


def rows_up(rows, up):
    return mm(rows[:, :384], up[:, :384]) + mm(rows[:, 384:], up[:, 384:])


def ffn_kernel(own, other, w0, w1, w3, up_2, down_2, keep, send):
    rows = all_rows((own, other))
    total = 0.0
    for up, down in shards(w0, w1, w3, up_2, down_2):
        total = total + mm(gelu(rows_up(rows, up)).astype(BF), down)
    keep[...] = total[:64]
    send[...] = total[64:].astype(BF)


def ffn_back_kernel(own, other, g_own, g_other, w0, w1, w3, up_2, down_2, keep, send):
    rows = all_rows((own, other))
    grad = all_rows((g_own, g_other))
    left = right = 0.0
    for up, down in shards(w0, w1, w3, up_2, down_2):
        slope = gelu_slope(rows_up(rows, up))
        pre = (mm_nt(grad, down) * slope).astype(BF)
        left = left + mm_nt(pre, up[:, :384])
        right = right + mm_nt(pre, up[:, 384:])
    total = jnp.concatenate([left, right], axis=1)
    keep[...] = total[:64]
    send[...] = total[64:].astype(BF)


def turn_kernel(base, keep, got, cot, norm, decoded, grad, low):
    values = base[...] + keep[...] + got[...].astype(F32)
    unit, inv = normed(values)
    gain = norm[2, 0:1]
    decoded[...] = (unit * gain + norm[2, 1:2]).astype(BF)
    up = cot[...].astype(F32)
    scaled = up * gain
    inner = jnp.mean(scaled * unit, axis=-1, keepdims=True)
    back = inv * (scaled - jnp.mean(scaled, axis=-1, keepdims=True) - unit * inner)
    grad[0:64] = back
    grad[64:72] = below(jnp.concatenate([jnp.sum(up * unit, axis=0, keepdims=True), jnp.sum(up, axis=0, keepdims=True)], axis=0))
    low[...] = back.astype(BF)


def below(*pairs):
    blank = jnp.zeros((8 - 2 * len(pairs), 768), F32)
    return jnp.concatenate([*pairs, blank], axis=0)


def ffn_norm_back_kernel(base, keep, got, values, norm, grad, low):
    up = base[0:64] + keep[...] + got[...].astype(F32)
    back, sums = norm_backward(up, values[...], norm[1, 0:1])
    grad[0:64] = back
    grad[64:72] = below(sums, base[64:66])
    low[...] = back.astype(BF)


def add_core_kernel(keep, got, out_0, out_1):
    total = (keep[...].astype(F32) + got[...].astype(F32)).astype(BF)
    out_0[...] = total[0]
    out_1[...] = total[1]


def add_core_self_kernel(keep, got, own, send):
    total = keep[...].astype(F32) + got[...].astype(F32)
    own[...] = total[0]
    send[...] = total[1].astype(BF)


def project_back_kernel(at, m0, m1, grad_q, w_cross, grad_pairs, *chunks):
    total = (m0[...].astype(F32) + m1[...].astype(F32)).astype(BF)
    grad_pairs[...] = total
    mine = jnp.concatenate([grad_q[...], jnp.zeros((256, 192), BF)], axis=1)
    mine = pick(at[0], mine.astype(F32), total.astype(F32)).astype(BF)
    put_chunks(mm(mine, w_cross[...]), chunks)


def memory_back_kernel(at, r0, r1, r2, r3, values, norm, in_d, in_e, grad_d, total, grad, low, both):
    up = add_chunks((r0, r1, r2, r3))
    total[...] = up
    back, sums = norm_backward(up, values[...], norm[2, 0:1])
    grad[0:64] = back
    grad[64:72] = below(sums)
    low[...] = back.astype(BF)
    both[0:64] = pick(at[0], in_d[...].astype(F32), in_e[...].astype(F32)).astype(BF)
    both[64:128] = pick(at[0], grad_d[...].astype(F32), back).astype(BF)


def first_norm_back_kernel(at, grad_e, keep, got, grad_d, low_sum, values, norm, grad, low):
    enc = grad_e[0:64] + keep[...] + got[...].astype(F32)
    up = pick(at[0], grad_d[0:64] + low_sum[...], enc)
    back, sums = norm_backward(up, values[...], norm[0, 0:1])
    low[...] = back.astype(BF)
    grad[0:64] = back
    grad[64:72] = below(sums, grad_d[64:66], pick(at[0], grad_d[66:68], grad_e[64:66]))


def entry_back_kernel(grad_q, own, got, w_in, packed, *chunks):
    kv = (own[...] + got[...].astype(F32)).astype(BF)
    packed[...] = jnp.concatenate([grad_q[...], kv], axis=1)
    put_chunks(mm(packed[...], w_in[...]), chunks)


def last_norm_back_kernel(at, r0, r1, r2, r3, base, tokens, norm, decoded, memory_sums, out):
    up = base[0:64] + add_chunks((r0, r1, r2, r3))
    back, sums = norm_backward(up, tokens[...].astype(F32), norm[1, 0:1])
    out[0:64] = pick(at[0], up, back).astype(BF)
    memory = norm_forward(memory_sums[...], norm[2, 0:1], norm[2, 1:2])
    out[64:128] = pick(at[0], decoded[...].astype(F32), memory).astype(BF)
    pairs = below(base[64:66], pick(at[0], base[66:68], sums), base[68:70])
    out[128:144] = two_parts(pairs)


def two_parts(values):
    high = values.astype(BF).astype(F32)
    return jnp.concatenate([high, values - high], axis=0).astype(BF)


def one_part(rows):
    rows = rows.astype(F32)
    return rows[:8] + rows[8:]


def collect_kernel(at, p0, p1, p2, p3, sums):
    parts = jnp.zeros((4, 8, 768), F32)
    place = lax.broadcasted_iota(I32, (4, 8, 768), 0)
    for j, ref in enumerate((p0, p1, p2, p3)):
        parts = jnp.where(place == ((at[4] + j) & 3), one_part(ref[128:144])[None], parts)
    sums[...] = (parts[0] + parts[1]) + (parts[2] + parts[3])


def rows_pack_kernel(at, p0, p1, p2, p3, chunks):
    for j, ref in enumerate((p0, p1, p2, p3)):
        chunks[(at[4] + j) & 3] = ref[0:128]


def rows_out_kernel(chunks, grads, outs):
    for micro in range(4):
        grads[micro] = chunks[micro, 0:64].astype(F32)
        outs[micro] = chunks[micro, 64:128]


def pack_kernel(sums, xh_sums, own, got, chunks):
    norms = two_parts(sums[...] + xh_sums[...])
    total = (own[...].astype(F32) + got[...].astype(F32)).astype(BF)
    for y in range(4):
        chunks[y, 0:16] = norms
        chunks[y, 16:112] = total


def unpack_kernel(chunks, norms, half):
    for y in range(4):
        half[96 * y : 96 * y + 96] = chunks[y, 16:112]
    parts = [one_part(chunks[y, 0:16]) for y in range(4)]
    norms[...] = (parts[0] + parts[1]) + (parts[2] + parts[3])


def split_core(full, at, keep, send):
    half = keep.shape[0]
    keep[...] = full[pl.ds(pl.multiple_of(at[3] * half, 16), half)]
    send[...] = full[pl.ds(pl.multiple_of((1 - at[3]) * half, 16), half)]


def ffn_weights_kernel(at, *refs):
    late, passed, crossed = (refs[4 * i : 4 * i + 4] for i in range(3))
    grad_pairs, grad_q, mixed, w_up, w_down, keep, send, full = refs[12:]
    flag = at[0]

    def choose(one, zero):
        return pick(flag, one.astype(F32), zero.astype(F32)).astype(BF)

    rows = all_rows(late, 0)
    grad = all_rows(late, 1)
    first = all_rows(passed)
    full[1536:1728] = mm_tn(choose(grad_q[...], grad_pairs[:, :192]), first).astype(BF)
    full[1728:1920] = mm_tn(choose(mixed[...], grad_pairs[:, 192:]), choose(all_rows(crossed), first)).astype(BF)
    pre = mm(rows, w_up[...])
    full[768:1536] = mm_tn(gelu(pre).astype(BF), grad).astype(BF)
    grad_pre = (mm_nt(grad, w_down[...]) * gelu_slope(pre)).astype(BF)
    full[0:768] = mm_tn(rows, grad_pre).astype(BF)
    split_core(full, at, keep, send)


def attn_weights_kernel(at, low, packed, mixed, g0, g1, g2, g3, keep, send, full):
    full[576:768] = mm_tn(mixed[...], all_rows((g0, g1, g2, g3), 0)).astype(BF)
    full[0:576] = mm_tn(packed[...], low[...]).astype(BF)
    split_core(full, at, keep, send)


def add_two_kernel(keep, got, out):
    rows = out.shape[1]
    for y in range(4):
        cut = slice(rows * y, rows * y + rows)
        out[y] = (keep[cut].astype(F32) + got[cut].astype(F32)).astype(BF)


def add_four_kernel(parts, out):
    total = (parts[0].astype(F32) + parts[1].astype(F32)) + (parts[2].astype(F32) + parts[3].astype(F32))
    out[...] = total.astype(out.dtype)


def add_all_kernel(*refs):
    total = refs[0][...].astype(F32)
    for ref in refs[1:-1]:
        total = total + ref[...].astype(F32)
    refs[-1][...] = total.astype(refs[-1].dtype)


def join_y_kernel(at, t0, t1, t2, t3, half):
    rows = t0.shape[0]
    for j, ref in enumerate((t0, t1, t2, t3)):
        half[pl.ds(pl.multiple_of(((at[2] + j) & 3) * rows, 16), rows)] = ref[...]


def join_core(at, own, got, full):
    half = own.shape[0]
    full[pl.ds(pl.multiple_of(at[3] * half, 16), half)] = own[...]
    full[pl.ds(pl.multiple_of((1 - at[3]) * half, 16), half)] = got[...]


def ffn_final_kernel(at, own, got, up, down, cross, full):
    join_core(at, own, got, full)
    up[...] = full[0:768].astype(F32)
    down[...] = full[768:1536].astype(F32)
    cross[...] = full[1536:1920].astype(F32)


def attn_final_kernel(at, own, got, grad_in, grad_out, full):
    join_core(at, own, got, full)
    grad_in[...] = full[0:576].astype(F32)
    grad_out[...] = full[576:768].astype(F32)


def reduce_y(keep, got, after=()):
    rows, cols = keep.shape
    (total,) = call(add_two_kernel, [((4, rows // 4, cols), BF)], keep, got, after=after)
    return total, lax.all_to_all(total, "y", 0, 0)


def add_four(parts, after=()):
    return call(add_four_kernel, [(parts.shape[1:], BF)], parts, after=after)[0]


def add_parts(parts, after=()):
    return call(add_all_kernel, [(parts[0].shape, BF)], *parts, after=after)[0]


KIND = {ffn_final_kernel: LONG, attn_weights_kernel: COST, entry_back_kernel: COST}
TAIL = (
    last_norm_back_kernel,
    collect_kernel,
    pack_kernel,
    rows_pack_kernel,
    rows_out_kernel,
    add_two_kernel,
    add_four_kernel,
    add_all_kernel,
    join_y_kernel,
    unpack_kernel,
)


def add_sums(one, two):
    return call(add_all_kernel, [((8, 768), F32)], one, two)[0]


def gather_y(at, total, after=()):
    parts = [total] + [shift(total, "y", -j) for j in range(1, 4)]
    rows, cols = total.shape
    return call(join_y_kernel, [((rows * 4, cols), BF)], *parts, scalars=(at,), after=after)[0]


def halves(at, w_up, w_down):
    def body(at, w_up, w_down, both, sems):
        first = pl.multiple_of(at[3] * 384, 128)
        copies = [
            pltpu.make_async_copy(w_up.at[0:384, pl.ds(first, 384)], both.at[0:384, 0:384], sems.at[0]),
            pltpu.make_async_copy(w_up.at[384:768, pl.ds(first, 384)], both.at[0:384, 384:768], sems.at[1]),
            pltpu.make_async_copy(w_down.at[pl.ds(first, 384)], both.at[384:768], sems.at[2]),
        ]
        for copy in copies:
            copy.start()
        for copy in copies:
            copy.wait()

    return pl.pallas_call(
        body,
        out_shape=jax.ShapeDtypeStruct((768, 768), BF),
        in_specs=[SMEM, HBM, HBM],
        out_specs=VMEM,
        scratch_shapes=[pltpu.SemaphoreType.DMA((3,))],
        cost_estimate=COST,
        name="halves_kernel",
    )(at, w_up, w_down)


def cut(left, right, after):
    def body(left, right, *refs):
        cut_kernel(left, right, *refs[len(after) :])

    return pl.pallas_call(
        body,
        out_shape=[jax.ShapeDtypeStruct((384, 768), BF)] * 2,
        in_specs=[HBM] * 2 + [ANY] * len(after),
        out_specs=[VMEM] * 2,
        scratch_shapes=[pltpu.SemaphoreType.DMA((2,))],
        cost_estimate=COST,
        name="cut_kernel",
    )(left, right, *after)


def per_device(tokens, segments, cotangent, attn_in, attn_out, ffn_in, ffn_out, cross_proj, norms):
    w_in = Far(jnp.transpose(attn_in[0], (1, 2, 0)).reshape(576, 768))
    w_out = Far(attn_out[0])
    w_up = ffn_in[0]
    w_down = ffn_out[0]
    w_cross = Far(jnp.transpose(cross_proj[0], (1, 2, 0)).reshape(384, 768))
    norm = norms[0]
    sec = lax.axis_index("section")
    x_at = lax.axis_index("xh")
    y_at = lax.axis_index("y")
    c_at = lax.axis_index("core")
    z_at = lax.axis_index("tensor")
    dec = sec == 1
    at = jnp.stack([sec, x_at, y_at, c_at, z_at]).astype(I32)
    here = (at,)

    arrived = lax.all_to_all(tokens[0, :, 0], "y", 0, 0)
    seg_micro = lax.dynamic_index_in_dim(segments[:, :, 0], y_at, 1, keepdims=False)
    ends = jnp.sum((seg_micro[:, None, :] <= jnp.arange(3, dtype=I32)[None, :, None]).astype(I32), axis=2)
    places = (at, ends)

    w_0 = halves(at, w_up, w_down)
    w_3, w_1 = shift(w_0, "tensor", 1), shift(w_0, "tensor", -1)

    entry_low, tok_own, queries, kv = call(
        entry_kernel,
        [far(((256, 768), BF)), far(ROWS_B), ((256, 192), BF), ((256, 384), BF)],
        arrived,
        norm,
        w_in,
        scalars=here,
    )
    cot_pairs = [(a * 4 + b, b * 4 + a) for a in range(4) for b in range(4)]
    cot_send = lax.dynamic_index_in_dim(cotangent[:, 0], z_at, 0, keepdims=False)
    cot_own = lax.ppermute(cot_send, ("y", "tensor"), cot_pairs)
    kv_x = shift(kv, "xh", 1)
    self_kv = (kv, swap_core(kv), kv_x, swap_core(kv_x))
    mixed, *chunks = call(
        attend_kernel, [far(((256, 192), BF))] + CHUNKS, queries, *self_kv, w_out, scalars=places, after=(cot_own,), cross=False
    )
    up_send, down_send = cut(w_3, w_1, (kv,))
    weights = [Far(w) for w in (w_0, w_1, w_3, shift(up_send, "tensor", 1), shift(down_send, "tensor", -1))]
    sums0, after_self_low = call(
        first_norm_kernel, [far(ROWS_F), ROWS_B], Far(tok_own), *scatter_z(chunks), norm, scalars=here
    )

    after_self_other = swap_core(after_self_low)
    keep, send = call(ffn_kernel, [ROWS_F, ROWS_B], after_self_low, after_self_other, *weights)
    sums2, passed = call(
        memory_kernel, [far(ROWS_F), ROWS_B], Far(sums0), keep, swap_core(send), norm, after_self_low, scalars=here
    )
    passed_all = gather_z(passed)
    (pairs,) = call(pairs_kernel, [((256, 384), BF)], *passed_all, w_cross)
    m0 = lax.ppermute(pairs, ("section", "xh"), section_pairs(0, 1, 0))
    m1 = lax.ppermute(pairs, ("section", "xh"), section_pairs(0, 1, 1))
    memory_kv = (m0, swap_core(m0), m1, swap_core(m1))
    (cross_q,) = call(query_kernel, [((256, 192), BF)], *passed_all, w_cross, after=(pairs,))

    mixed_cross, *chunks = call(
        attend_kernel, [far(((256, 192), BF))] + CHUNKS, cross_q, *memory_kv, w_cross, scalars=places, cross=True
    )
    sums1, after_cross, after_cross_low = call(
        cross_norm_kernel, [ROWS_F, ROWS_F, ROWS_B], Far(sums0), *scatter_z(chunks), norm
    )
    after_cross_other = swap_core(after_cross_low)
    keep, send = call(ffn_kernel, [ROWS_F, ROWS_B], after_cross_low, after_cross_other, *weights)
    decoded, grad_d2, grad_ffn_d = call(
        turn_kernel, [far(ROWS_B), MORE_F, ROWS_B], after_cross, keep, swap_core(send), Far(cot_own), norm
    )

    keep, send = call(
        ffn_back_kernel,
        [ROWS_F, ROWS_B],
        after_cross_low,
        after_cross_other,
        grad_ffn_d,
        swap_core(grad_ffn_d),
        *weights,
    )
    grad_d1, grad_d1_low = call(
        ffn_norm_back_kernel, [far(MORE_F), ROWS_B], grad_d2, keep, swap_core(send), sums1, norm
    )
    grad_crossed_all = gather_z(grad_d1_low)
    pair_b = ((2, 256, 384), BF)
    grad_q_cross, keep, send = call(
        attend_back_kernel,
        [((256, 192), BF), pair_b, pair_b],
        *grad_crossed_all,
        cross_q,
        *memory_kv,
        w_cross,
        scalars=places,
        cross=True,
    )
    to_0, to_1 = call(add_core_kernel, [((256, 384), BF)] * 2, keep, swap_core(send))
    g0 = lax.ppermute(to_0, ("section", "xh"), section_pairs(1, 0, 0))
    g1 = lax.ppermute(to_1, ("section", "xh"), section_pairs(1, 0, 1))

    grad_pairs, *chunks = call(
        project_back_kernel, [((256, 384), BF)] + CHUNKS, g0, g1, grad_q_cross, w_cross, scalars=here
    )
    low_sum, grad_e2, grad_ffn_e, both = call(
        memory_back_kernel,
        [ROWS_F, MORE_F, ROWS_B, BOTH_B],
        *scatter_z(chunks),
        Far(sums2),
        norm,
        after_cross_low,
        after_self_low,
        grad_ffn_d,
        scalars=here,
    )
    both_all = gather_z(both)
    keep, send = call(
        ffn_back_kernel,
        [ROWS_F, ROWS_B],
        after_self_low,
        after_self_other,
        grad_ffn_e,
        swap_core(grad_ffn_e),
        *weights,
    )
    grad_0, grad_0_low = call(
        first_norm_back_kernel,
        [far(MORE_F), ROWS_B],
        grad_e2,
        keep,
        swap_core(send),
        Far(grad_d1),
        low_sum,
        Far(sums0),
        norm,
        scalars=here,
    )
    grad_sa_all = gather_z(grad_0_low)

    half = ((960, 768), BF)
    w_keep, w_send = call(
        ffn_weights_kernel,
        [half, half],
        *both_all,
        *passed_all,
        *grad_crossed_all,
        grad_pairs,
        grad_q_cross,
        Far(mixed_cross),
        Far(w_up),
        Far(w_down),
        scalars=here,
        scratch=[((1920, 768), BF)],
        after=grad_sa_all,
    )

    grad_q, keep, send = call(
        attend_back_kernel,
        [((256, 192), BF), pair_b, pair_b],
        *grad_sa_all,
        queries,
        *self_kv,
        w_out,
        scalars=places,
        after=(w_keep,),
        cross=False,
    )
    own_kv, send_kv = call(
        add_core_self_kernel, [((256, 384), F32), ((256, 384), BF)], keep, swap_core(send)
    )
    w_sent, w_parts = reduce_y(w_keep, swap_core(w_send), after=(own_kv, grad_q))
    grad_packed, *chunks = call(
        entry_back_kernel,
        [((256, 576), BF)] + CHUNKS,
        grad_q,
        own_kv,
        shift(send_kv, "xh", 1),
        w_in,
        after=(w_sent,),
    )
    got_chunks = scatter_z(chunks)
    half = ((384, 768), BF)
    a_keep, a_send = call(
        attn_weights_kernel,
        [half, half],
        Far(entry_low),
        grad_packed,
        Far(mixed),
        *grad_sa_all,
        scalars=here,
        scratch=[((768, 768), BF)],
    )
    (grad_own,) = call(
        last_norm_back_kernel,
        [((144, 768), BF)],
        *got_chunks,
        Far(grad_0),
        Far(tok_own),
        norm,
        Far(decoded),
        Far(sums2),
        scalars=here,
        after=(a_keep,),
    )
    own_all = gather_z(grad_own)
    a_sent, a_parts = reduce_y(a_keep, swap_core(a_send), after=(grad_own,))
    w_piece = add_four(w_parts, after=(grad_own,))
    w_total = add_parts([w_piece, shift(w_piece, "xh", 1)], after=own_all[1:])
    a_piece = add_four(a_parts, after=(grad_own,))
    a_got = shift(a_piece, "xh", 1)
    (row_chunks,) = call(rows_pack_kernel, [((4, 128, 768), BF)], *own_all, scalars=here)
    token_grads, outputs = call(
        rows_out_kernel,
        [far(((4, 64, 768), F32)), far(((4, 64, 768), BF))],
        lax.all_to_all(row_chunks, "y", 0, 0),
    )
    (sums,) = call(collect_kernel, [((8, 768), F32)], *own_all, scalars=here, after=(w_total,))
    sums = add_sums(sums, swap_core(sums))
    xh_sums = shift(sums, "xh", 1)
    (packed_out,) = call(
        pack_kernel,
        [((4, 112, 768), BF)],
        sums,
        xh_sums,
        a_piece,
        a_got,
    )
    unpacked = lax.all_to_all(packed_out, "y", 0, 0)
    w_half = gather_y(at, w_total, after=(packed_out, token_grads))
    grad_up, grad_down, grad_cross = call(
        ffn_final_kernel,
        [far(((768, 768), F32)), far(((768, 768), F32)), far(((384, 768), F32))],
        w_half,
        swap_core(w_half),
        scalars=here,
        scratch=[((1920, 768), BF)],
    )
    norm_sums, a_half = call(
        unpack_kernel,
        [far(((8, 768), F32)), ((384, 768), BF)],
        unpacked,
        after=(grad_up,),
    )
    grad_in, grad_out = call(
        attn_final_kernel,
        [far(((576, 768), F32)), far(((192, 768), F32))],
        a_half,
        swap_core(a_half),
        scalars=here,
        scratch=[((768, 768), BF)],
    )
    return (
        outputs[None, :, None],
        token_grads[None, :, None],
        jnp.transpose(grad_in.reshape(3, 192, 768), (2, 0, 1))[None],
        grad_out[None],
        grad_up[None],
        grad_down[None],
        jnp.transpose(grad_cross.reshape(2, 192, 768), (2, 0, 1))[None],
        norm_sums[:6].reshape(1, 3, 2, 768),
    )


def solution(mesh):
    fine = Mesh(mesh.devices.reshape(2, 2, 4, 2, 4), ("section", "xh", "y", "core", "tensor"))
    dp = ("xh", "y", "core")
    weights = (
        P("section", None, None, "tensor"),
        P("section", "tensor", None),
        P("section", None, "tensor"),
        P("section", "tensor", None),
        P("section", None, None, "tensor"),
        P("section", None, None, None),
    )
    rows = P("section", None, None, dp, None)
    return jax.shard_map(
        per_device,
        mesh=fine,
        in_specs=(rows, P(), P(None, None, dp, None)) + weights,
        out_specs=(rows, rows) + weights,
        check_vma=False,
    )
```
